32 devices in a mesh: group: 2 (over x), trade: 16 (over z, y, core).
Axes of the slice: x: 2, y: 2, z: 4, core: 2. Of those that a mesh axis runs over, the one named last changes fastest.
Arguments:
- factors: bfloat16 [128, 128], P(('group', 'trade')), parts along dimension 0, may hold values from -6 to 6
- loadings: float32 [32, 16], replicated, may hold values from -1.5 to 1.5
- trade_coef: bfloat16 [65536, 256], P(('group', 'trade')), parts along dimension 0, may hold values from -0.75 to 0.75
- basis_size: int32 [65536], P(('group', 'trade')), parts along dimension 0, may hold values from 4 to 32
- set_ids: int32 [65536], P(('group', 'trade')), parts along dimension 0, may hold values from 0 to 31
- live_count: int32 [32], P(('group', 'trade')), parts along dimension 0, may hold values from 1 to 2047, as said below
- netting_row: int32 [64], P('group'), parts along dimension 0, may hold values from 0 to 31, each once
- threshold: float32 [64], P(('group', 'trade')), parts along dimension 0, may hold values from 0.5 to 8
- margin_start: float32 [64, 64], P(('group', 'trade')), parts along dimension 0, may hold values from 0 to 3
Outputs:
- expected: float32 [64, 8], P(('group', 'trade')), parts along dimension 0
The draws below stay inside these ranges and needn't reach their ends.
There are 2 independent parts, one for each index of `group`. The reference program is written for one: setup_inputs(seed, part) draws one part's arguments, and reference() takes and returns one part's arrays. A program takes and returns all parts, laid end to end along the dimension named above; an argument that names none is the same for every part. Nothing has to cross between parts.
Inputs may be any that keep to these rules, and one draw needn't show every extreme that they name: `live_count`: blocks b and b + 8 hold exactly 2048 live trades together.
All inputs are finite; a program needn't handle non-finite values.
Results may differ from the reference program's by a relative error of at most 0.00035.
Values may be sent and summed in bfloat16 or wider, within the bound.
No kernel may reach another device: no remote copies, remote signals or barrier semaphores. Data moves between devices by JAX's collectives and lax.ppermute only.
A program may use at most 64 MiB of HBM per device.

```python
import math
import jax
import jax.numpy as jnp
import numpy as np
from jax import lax

F = 16
K = 32
DATES = 8
LAG = 2
AVG = 1024
SLOTS = 2048
BLOCKS = 16
TRADES = 32768
P_SIZE = 64
NS = 32


def draw_live_count(key, part):
    half_blocks = BLOCKS // 2
    first_key, second_key = jax.random.split(jax.random.fold_in(key, 11))
    lower = jax.random.randint(first_key, (half_blocks,), 1, 2 * AVG, dtype=jnp.int32)
    heavy = jax.random.randint(second_key, (), 0, half_blocks, dtype=jnp.int32)
    lower = jnp.where(jnp.arange(half_blocks, dtype=jnp.int32) == heavy, 2 * AVG - 1, lower)
    return jnp.concatenate([lower, 2 * AVG - lower]).astype(jnp.int32)


def set_ends(result, rng, smallest, top_value):
    spot = [jax.random.randint(jax.random.fold_in(rng, axis), (), 0, length) for axis, length in enumerate(result.shape)]
    widest = result.shape.index(max(result.shape))
    neighbour = spot[:widest] + [(spot[widest] + 1) % result.shape[widest]] + spot[widest + 1:]
    return result.at[tuple(spot)].set(smallest).at[tuple(neighbour)].set(top_value)


def block_levels(own_key, shape, shards, smallest, top_value):
    level = 1.0
    for axis_at, parts in shards:
        draws = jax.random.uniform(jax.random.fold_in(jax.random.fold_in(own_key, 6), axis_at), (parts,), jnp.float32, smallest / len(shards), top_value / len(shards))
        level = level * jnp.repeat(jnp.exp(draws), shape[axis_at] // parts).reshape((-1,) + (1,) * (len(shape) - 1 - axis_at))
    return level


def rank_table(count, slope):
    portions = [(1 << 20) // math.isqrt(standing ** slope) + 1 for standing in range(1, count + 1)]
    spread = 1 + sum(portions) // (1 << 30)
    return np.cumsum(np.array([max(1, weight // spread) for weight in portions]))


def ranked_ids(stream_key, extent, number_of, lean):
    listing = rank_table(number_of, lean)
    lot = jax.random.randint(jax.random.fold_in(stream_key, 1), extent, 0, int(listing[number_of - 1]))
    grade = jnp.searchsorted(jnp.asarray(listing, jnp.int32), lot, side="right")
    return jax.random.permutation(jax.random.fold_in(stream_key, 2), number_of)[grade].astype(jnp.int32)


def scatter_about(key, dims, width, most, shards=(), kind=jnp.bfloat16):
    level = block_levels(key, dims, shards, -0.22, 0.18) if shards else 1.0
    entries = jax.random.normal(key, dims, jnp.float32) * width * level
    return jnp.minimum(jnp.maximum(entries, -most), most).astype(kind)


def setup_inputs(seed: int = 0, part: int = 0) -> dict:
    splits = jax.random.split(jax.random.key(seed), 10)
    own_keys = jax.random.split(jax.random.fold_in(splits[9], part), 10)
    factors = scatter_about(own_keys[0], (P_SIZE, DATES * F), 1.0, 6.0, ((0, 16),))
    loadings = scatter_about(splits[1], (K, F), F ** -0.5, 1.5, (), jnp.float32)
    trade_coef = scatter_about(own_keys[2], (TRADES, DATES * K), 0.05, 0.75, ((0, 16),))
    basis_size = set_ends(jax.random.randint(own_keys[3], (TRADES,), 4, K + 1), jax.random.fold_in(own_keys[3], 1), 4, K).astype(jnp.int32)
    set_ids = set_ends(ranked_ids(own_keys[4], (TRADES,), NS, 1), jax.random.fold_in(own_keys[4], 3), 0, NS - 1).astype(jnp.int32)
    live_count = draw_live_count(jax.random.fold_in(jax.random.fold_in(splits[9], part), 71), part)
    netting_row = jax.random.permutation(own_keys[6], NS).astype(jnp.int32)
    threshold = jnp.clip(jnp.exp(math.log(8.0) - 2.7725887 * jax.random.uniform(own_keys[7], (NS,), jnp.float32) ** block_levels(own_keys[7], (NS,), ((0, 16),), -0.2, 0.2)), 0.5, 8.0)
    margin_start = jnp.clip(3.0 * jax.random.uniform(own_keys[8], (NS, P_SIZE), jnp.float32) ** block_levels(own_keys[8], (NS, P_SIZE), ((0, 16),), -0.2, 0.2), 0.0, 3.0)
    return {"factors": factors, "loadings": loadings, "trade_coef": trade_coef, "basis_size": basis_size, "set_ids": set_ids, "live_count": live_count, "netting_row": netting_row, "threshold": threshold, "margin_start": margin_start}


def reference(factors, loadings, trade_coef, basis_size, set_ids, live_count, netting_row, threshold, margin_start):
    path_total = factors.shape[0]
    set_total = netting_row.shape[0]
    factor_cube = factors.astype(jnp.float32).reshape(path_total, DATES, F)
    basis_table = jnp.einsum("pdf,kf->pdk", factor_cube, loadings, precision=lax.Precision.HIGHEST)
    basis_table = jnp.tanh(basis_table).astype(jnp.bfloat16)
    basis_wide = basis_table.astype(jnp.float32)
    trade_rows = netting_row[set_ids].astype(jnp.int32)
    basis_index = jnp.arange(K, dtype=jnp.int32)
    slot_index = jnp.arange(SLOTS, dtype=jnp.int32)

    def add_block(block_index, running):
        first_row = (block_index * SLOTS).astype(jnp.int32)
        coef_block = lax.dynamic_slice_in_dim(trade_coef, first_row, SLOTS, 0).reshape(SLOTS, DATES, K)
        sizes_block = lax.dynamic_slice_in_dim(basis_size, first_row, SLOTS, 0)
        rows_block = lax.dynamic_slice_in_dim(trade_rows, first_row, SLOTS, 0)
        live_now = live_count[block_index]
        keep_mask = (basis_index[None, :] < sizes_block[:, None]) & (slot_index < live_now)[:, None]
        coef_used = jnp.where(keep_mask[:, None, :], coef_block, jnp.zeros_like(coef_block)).astype(jnp.bfloat16)
        values = jnp.einsum("tdk,pdk->tdp", coef_used.astype(jnp.float32), basis_wide)
        values = values.astype(jnp.bfloat16).astype(jnp.float32).reshape(SLOTS, DATES * path_total)
        return running + jax.ops.segment_sum(values, rows_block, num_segments=set_total)

    running = jnp.zeros((set_total, DATES * path_total), jnp.float32)
    running = lax.fori_loop(0, BLOCKS, add_block, running)
    netted = running.reshape(set_total, DATES, path_total)
    margin = jnp.maximum(netted[:, : DATES - LAG] - threshold[:, None, None], 0.0)
    held = jnp.broadcast_to(margin_start[:, None, :], (set_total, LAG, path_total))
    collateral = jnp.concatenate([held, margin], axis=1)
    shortfall = jnp.maximum(netted - collateral, 0.0)
    return jnp.sum(shortfall, axis=2) / path_total
```

```python
import jax
import jax.numpy as jnp
from jax import lax
from jax.sharding import PartitionSpec as P

F = 16
K = 32
DATES = 8
LAG = 2


def swap(x, bit, count):
    return lax.ppermute(x, "trade", [(i, i ^ bit) for i in range(count)])


def gather_paths(x, count):
    me = lax.axis_index("trade")
    bit = 1
    while bit < count:
        other = swap(x, bit, count)
        upper = (me & bit) != 0
        x = jnp.concatenate([jnp.where(upper, other, x), jnp.where(upper, x, other)], axis=0)
        bit *= 2
    return x


def bit_reversed(index, count):
    result = jnp.zeros_like(index)
    bit = 1
    while bit < count:
        result = result * 2 + (index & 1)
        index = index >> 1
        bit *= 2
    return result


def scatter_sums(x, count):
    bit = 1
    while bit < count:
        half = x.shape[0] // 2
        x = x[:half] + swap(x[half:], bit, count)
        bit *= 2
    return x


def body(
    factors,
    loadings,
    trade_coef,
    basis_size,
    set_ids,
    live_count,
    netting_row,
    threshold,
    margin_start,
    *,
    count,
):
    me = lax.axis_index("trade")
    own_rows = threshold.shape[0]
    set_total = netting_row.shape[0]
    slot_total = trade_coef.shape[0]

    coef_cube = trade_coef.reshape(slot_total, DATES, K)
    basis_index = jnp.arange(K, dtype=jnp.int32)
    keep_mask = basis_index[None, :] < basis_size[:, None]
    coef_used = jnp.where(keep_mask[:, None, :], coef_cube, jnp.zeros_like(coef_cube))

    place = jnp.arange(set_total, dtype=jnp.int32)
    row_at = (bit_reversed(place // own_rows, count) ^ me) * own_rows + place % own_rows
    set_at = jnp.sum(jnp.where(row_at[:, None] == netting_row[None, :], place[None, :], 0), axis=1)
    slot_index = jnp.arange(slot_total, dtype=jnp.int32)
    live = slot_index < live_count[0]
    onehot = ((set_ids[None, :] == set_at[:, None]) & live[None, :]).astype(jnp.bfloat16)

    paths = gather_paths(factors, count)
    path_total = paths.shape[0]
    factor_cube = paths.astype(jnp.float32).reshape(path_total, DATES, F)
    loaded = jnp.einsum("pdf,kf->pdk", factor_cube, loadings, precision=lax.Precision.HIGHEST)
    basis_table = jnp.tanh(loaded).astype(jnp.bfloat16)
    values = jnp.einsum("tdk,pdk->tdp", coef_used, basis_table, preferred_element_type=jnp.float32)
    values = values.astype(jnp.bfloat16).reshape(slot_total, DATES * path_total)
    netted = jnp.dot(onehot, values, preferred_element_type=jnp.float32)
    netted = scatter_sums(netted, count).reshape(own_rows, DATES, path_total)

    margin = jnp.maximum(netted[:, : DATES - LAG] - threshold[:, None, None], 0.0)
    held = jnp.broadcast_to(margin_start[:, None, :], (own_rows, LAG, path_total))
    collateral = jnp.concatenate([held, margin], axis=1)
    shortfall = jnp.sum(jnp.maximum(netted - collateral, 0.0), axis=2)
    return shortfall / path_total


def solution(mesh):
    count = mesh.shape["trade"]

    def local(*args):
        return body(*args, count=count)

    return jax.shard_map(
        local,
        mesh=mesh,
        in_specs=(
            P(("group", "trade"), None),
            P(),
            P(("group", "trade"), None),
            P(("group", "trade")),
            P(("group", "trade")),
            P(("group", "trade")),
            P("group"),
            P(("group", "trade")),
            P(("group", "trade"), None),
        ),
        out_specs=P(("group", "trade"), None),
        check_vma=False,
    )
```

```python
import jax
import jax.numpy as jnp
from jax import lax
from jax.sharding import PartitionSpec as P

F = 16
K = 32
DATES = 8
LAG = 2


def swap(x, bit, count):
    return lax.ppermute(x, "trade", [(i, i ^ (bit | 1)) for i in range(count)])


def gather_paths(x, count):
    me = lax.axis_index("trade")
    bit = 1
    while bit < count:
        other = swap(x, bit, count)
        upper = (me & bit) != 0
        x = jnp.concatenate([jnp.where(upper, other, x), jnp.where(upper, x, other)], axis=0)
        bit *= 2
    return x


def offsets(index, count):
    result = jnp.zeros_like(index)
    bit = 1
    top = count // 2
    while bit < count:
        result = result ^ jnp.where((index & top) != 0, bit | 1, 0)
        bit *= 2
        top //= 2
    return result


def scatter_sums(x, count):
    bit = 1
    while bit < count:
        half = x.shape[0] // 2
        x = x[:half] + swap(x[half:], bit, count)
        bit *= 2
    return x


def body(
    factors,
    loadings,
    trade_coef,
    basis_size,
    set_ids,
    live_count,
    netting_row,
    threshold,
    margin_start,
    *,
    count,
):
    me = lax.axis_index("trade")
    own_rows = threshold.shape[0]
    set_total = netting_row.shape[0]
    slot_total = trade_coef.shape[0]

    coef_cube = trade_coef.reshape(slot_total, DATES, K)
    basis_index = jnp.arange(K, dtype=jnp.int32)
    keep_mask = basis_index[None, :] < basis_size[:, None]
    coef_used = jnp.where(keep_mask[:, None, :], coef_cube, jnp.zeros_like(coef_cube))

    place = jnp.arange(set_total, dtype=jnp.int32)
    row_at = (offsets(place // own_rows, count) ^ me) * own_rows + place % own_rows
    set_at = jnp.sum(jnp.where(row_at[:, None] == netting_row[None, :], place[None, :], 0), axis=1)
    slot_index = jnp.arange(slot_total, dtype=jnp.int32)
    live = slot_index < live_count[0]
    onehot = ((set_ids[None, :] == set_at[:, None]) & live[None, :]).astype(jnp.bfloat16)

    paths = gather_paths(factors, count)
    path_total = paths.shape[0]
    factor_cube = paths.astype(jnp.float32).reshape(path_total, DATES, F)
    loaded = jnp.einsum("pdf,kf->pdk", factor_cube, loadings, precision=lax.Precision.HIGHEST)
    basis_table = jnp.tanh(loaded).astype(jnp.bfloat16)
    values = jnp.einsum("tdk,pdk->tdp", coef_used, basis_table, preferred_element_type=jnp.float32)
    values = values.astype(jnp.bfloat16).reshape(slot_total, DATES * path_total)
    netted = jnp.dot(onehot, values, preferred_element_type=jnp.float32)
    netted = scatter_sums(netted, count).reshape(own_rows, DATES, path_total)

    margin = jnp.maximum(netted[:, : DATES - LAG] - threshold[:, None, None], 0.0)
    held = jnp.broadcast_to(margin_start[:, None, :], (own_rows, LAG, path_total))
    collateral = jnp.concatenate([held, margin], axis=1)
    shortfall = jnp.sum(jnp.maximum(netted - collateral, 0.0), axis=2)
    return shortfall / path_total


def solution(mesh):
    count = mesh.shape["trade"]

    def local(*args):
        return body(*args, count=count)

    return jax.shard_map(
        local,
        mesh=mesh,
        in_specs=(
            P(("group", "trade"), None),
            P(),
            P(("group", "trade"), None),
            P(("group", "trade")),
            P(("group", "trade")),
            P(("group", "trade")),
            P("group"),
            P(("group", "trade")),
            P(("group", "trade"), None),
        ),
        out_specs=P(("group", "trade"), None),
        check_vma=False,
    )
```

```python
import jax
import jax.numpy as jnp
from jax import lax
from jax.experimental import pallas as pl
from jax.experimental.pallas import tpu as pltpu
from jax.sharding import PartitionSpec as P

F = 16
K = 32
DATES = 8
LAG = 2
LANES = 128
PATH_BLOCK = 32
SLOT_BLOCK = 1024
VMEM = pl.BlockSpec(memory_space=pltpu.VMEM)
SMEM = pl.BlockSpec(memory_space=pltpu.SMEM)


def call(kernel, outs, specs, flops, args):
    sizes = [a.size * a.dtype.itemsize for a in (*args, *outs)]
    return pl.pallas_call(
        kernel,
        out_shape=outs,
        in_specs=specs,
        out_specs=[VMEM] * len(outs),
        compiler_params=pltpu.CompilerParams(vmem_limit_bytes=24 * 2**20),
        cost_estimate=pl.CostEstimate(flops=flops, bytes_accessed=sum(sizes), transcendentals=0),
    )(*args)


def swap(x, bit, count):
    return lax.ppermute(x, "trade", [(i, i ^ (bit | 1)) for i in range(count)])


def join(own, other, bit):
    upper = (lax.axis_index("trade") & bit) != 0
    return jnp.concatenate([jnp.where(upper, other, own), jnp.where(upper, own, other)], axis=0)


def offsets(index, count):
    result = jnp.zeros_like(index)
    bit = 1
    top = count // 2
    while bit < count:
        result = result ^ jnp.where((index & top) != 0, bit | 1, 0)
        bit *= 2
        top //= 2
    return result


def scatter_sums(kept, sent, count):
    bit = 1
    while bit < count // 2:
        x = kept + swap(sent, bit, count)
        half = x.shape[0] // 2
        kept, sent = x[:half], x[half:]
        bit *= 2
    near = sent.shape[1] // 2
    return kept + swap(jnp.concatenate([sent[:, near:], sent[:, :near]], axis=1), bit, count)


def copy_kernel(factors_ref, own_ref):
    own_ref[...] = factors_ref[...]


def rows_kernel(
    count, me_ref, live_ref, limit_ref, loadings_ref, ids_ref, owner_ref, limits_ref, split_ref, onehot_ref
):
    own_rows = limits_ref.shape[0]
    for r in range(own_rows):
        limits_ref[r : r + 1, :] = jnp.full((1, LANES), limit_ref[r])
    set_total = owner_ref.shape[1]
    place = lax.broadcasted_iota(jnp.int32, (set_total, 1), 0)
    block = lax.shift_right_logical(place, own_rows.bit_length() - 1)
    row_at = (offsets(block, count) ^ me_ref[0]) * own_rows + (place & (own_rows - 1))
    sets = lax.broadcasted_iota(jnp.int32, (set_total, set_total), 1)
    set_at = jnp.sum(jnp.where(row_at == owner_ref[...], sets, 0), axis=1, keepdims=True)
    lane = lax.broadcasted_iota(jnp.int32, (1, LANES), 1)
    live = live_ref[0]
    for c in range(ids_ref.shape[0]):
        ids = jnp.where(lane + c * LANES < live, ids_ref[c : c + 1, :], -1)
        hit = jnp.where(ids == set_at, 1.0, 0.0)
        onehot_ref[:, c * LANES : (c + 1) * LANES] = hit.astype(jnp.bfloat16)
    tall = jnp.concatenate([loadings_ref[...].T] * DATES, axis=0)
    wide = jnp.concatenate([tall] * DATES, axis=1)
    row = lax.broadcasted_iota(jnp.int32, wide.shape, 0) // K
    column = lax.broadcasted_iota(jnp.int32, wide.shape, 1) // F
    rest = jnp.where(row == column, wide, 0.0)
    for i in range(3):
        part = rest.astype(jnp.bfloat16)
        split_ref[i] = part
        rest = rest - part.astype(jnp.float32)


def coef_kernel(coef_ref, size_ref, used_ref):
    sizes = size_ref[...].astype(jnp.float32).T
    width = coef_ref.shape[1]
    basis = (lax.broadcasted_iota(jnp.int32, (1, width), 1) & (K - 1)).astype(jnp.float32)
    for c in range(size_ref.shape[0]):
        rows = slice(c * LANES, (c + 1) * LANES)
        coef = coef_ref[rows, :].astype(jnp.float32)
        used_ref[rows, :] = jnp.where(basis < sizes[:, c : c + 1], coef, 0.0).astype(jnp.bfloat16)


def net_block(paths, split_ref, used_ref, onehot_ref):
    total = paths.shape[0]
    tiled = jnp.concatenate([paths] * DATES, axis=0)
    contract = (((1,), (1,)), ((), ()))
    loaded = sum(
        lax.dot_general(split_ref[i], tiled, contract, preferred_element_type=jnp.float32) for i in (2, 1, 0)
    )
    row = lax.broadcasted_iota(jnp.int32, loaded.shape, 0) // K
    column = lax.broadcasted_iota(jnp.int32, loaded.shape, 1) // total
    table = jnp.where(row == column, jnp.tanh(loaded), 0.0).astype(jnp.bfloat16)
    slots = used_ref.shape[0]
    step = min(SLOT_BLOCK, slots)
    result = jnp.zeros((onehot_ref.shape[0], DATES * total), jnp.float32)
    for at in range(0, slots, step):
        values = jnp.dot(used_ref[at : at + step, :], table, preferred_element_type=jnp.float32)
        values = values.astype(jnp.bfloat16)
        result = result + jnp.dot(onehot_ref[:, at : at + step], values, preferred_element_type=jnp.float32)
    return result


def near_kernel(paths_ref, split_ref, used_ref, onehot_ref, net_ref):
    block = min(PATH_BLOCK, paths_ref.shape[0])
    for b in range(paths_ref.shape[0] // block):
        net = net_block(paths_ref[b * block : (b + 1) * block, :], split_ref, used_ref, onehot_ref)
        net_ref[:, b * DATES * block : (b + 1) * DATES * block] = net


def far_kernel(paths_ref, split_ref, used_ref, onehot_ref, near_ref, kept_ref, sent_ref):
    half = kept_ref.shape[0]
    width = near_ref.shape[1]
    kept_ref[:, :width] = near_ref[:half, :]
    sent_ref[:, :width] = near_ref[half:, :]
    block = min(PATH_BLOCK, paths_ref.shape[0])
    for b in range(paths_ref.shape[0] // block):
        net = net_block(paths_ref[b * block : (b + 1) * block, :], split_ref, used_ref, onehot_ref)
        at = slice(width + b * DATES * block, width + (b + 1) * DATES * block)
        sent_ref[:, at] = net[half:, :]
        kept_ref[:, at] = net[:half, :]


def body(
    factors,
    loadings,
    trade_coef,
    basis_size,
    set_ids,
    live_count,
    netting_row,
    threshold,
    margin_start,
    *,
    count,
):
    me = lax.axis_index("trade")
    own_rows = threshold.shape[0]
    set_total = netting_row.shape[0]
    slot_total, width = trade_coef.shape
    shape = jax.ShapeDtypeStruct
    f32, bf16 = jnp.float32, jnp.bfloat16

    (own,) = call(copy_kernel, [shape(factors.shape, bf16)], [VMEM], 10**6, (factors,))
    near = join(own, swap(factors, 1, count), 1)
    sizes = basis_size.reshape(-1, LANES)
    sizes, near = lax.optimization_barrier((sizes, near))
    (used,) = call(coef_kernel, [shape(trade_coef.shape, bf16)], [VMEM, VMEM], 10**8, (trade_coef, sizes))
    near = join(near, swap(near, 2, count), 2)
    ids = set_ids.reshape(-1, LANES)
    ids, near = lax.optimization_barrier((ids, near))
    limits, split, onehot = call(
        lambda *refs: rows_kernel(count, *refs),
        [shape((own_rows, LANES), f32), shape((3, DATES * K, DATES * F), bf16), shape((set_total, slot_total), bf16)],
        [SMEM, SMEM, SMEM, VMEM, VMEM, VMEM],
        10**8,
        (me.astype(jnp.int32).reshape(1), live_count, threshold, loadings.T, ids, netting_row.reshape(1, -1)),
    )
    bit = 4
    while bit < count // 2:
        near = join(near, swap(near, bit, count), bit)
        bit *= 2
    far = swap(near, bit, count)
    side_total = near.shape[0]
    columns = DATES * side_total
    work = 2 * columns * slot_total * (width + set_total)
    (near_net,) = call(
        near_kernel, [shape((set_total, columns), f32)], [VMEM] * 4, work, (near, split, used, onehot)
    )
    kept, sent = call(
        far_kernel,
        [shape((set_total // 2, 2 * columns), f32)] * 2,
        [VMEM] * 5,
        work,
        (far, split, used, onehot, near_net),
    )
    netted = scatter_sums(kept, sent, count)

    upper = (me & (count // 2)) != 0
    flipped = jnp.concatenate([margin_start[:, side_total:], margin_start[:, :side_total]], axis=1)
    start = jnp.where(upper, flipped, margin_start)

    block = min(PATH_BLOCK, side_total)
    netted = netted.reshape(own_rows, -1, DATES, block)
    start = start.reshape(own_rows, -1, 1, block)
    margin = jnp.maximum(netted[:, :, : DATES - LAG] - limits[:, :1, None, None], 0.0)
    held = jnp.broadcast_to(start, (own_rows, start.shape[1], LAG, block))
    collateral = jnp.concatenate([held, margin], axis=2)
    shortfall = jnp.sum(jnp.maximum(netted - collateral, 0.0), axis=(1, 3))
    return shortfall / (2 * side_total)


def solution(mesh):
    count = mesh.shape["trade"]

    def local(*args):
        return body(*args, count=count)

    return jax.shard_map(
        local,
        mesh=mesh,
        in_specs=(
            P(("group", "trade"), None),
            P(),
            P(("group", "trade"), None),
            P(("group", "trade")),
            P(("group", "trade")),
            P(("group", "trade")),
            P("group"),
            P(("group", "trade")),
            P(("group", "trade"), None),
        ),
        out_specs=P(("group", "trade"), None),
        check_vma=False,
    )
```

```python
import jax
import jax.numpy as jnp
from jax import lax
from jax.experimental import pallas as pl
from jax.experimental.pallas import tpu as pltpu
from jax.sharding import PartitionSpec as P

F = 16
K = 32
DATES = 8
LAG = 2
LANES = 128
PATH_BLOCK = 32
SLOT_BLOCK = 512
VMEM = pl.BlockSpec(memory_space=pltpu.VMEM)
SMEM = pl.BlockSpec(memory_space=pltpu.SMEM)
HBM = pl.BlockSpec(memory_space=pltpu.HBM)
PARTS = 4


def call(kernel, outs, specs, flops, args, scratch=()):
    sizes = [a.size * a.dtype.itemsize for a in (*args, *outs)]
    return pl.pallas_call(
        kernel,
        out_shape=outs,
        in_specs=specs,
        out_specs=[VMEM] * len(outs),
        scratch_shapes=scratch,
        compiler_params=pltpu.CompilerParams(vmem_limit_bytes=24 * 2**20),
        cost_estimate=pl.CostEstimate(flops=flops, bytes_accessed=sum(sizes), transcendentals=0),
    )(*args)


def in_hbm(x):
    return pltpu.with_memory_space_constraint(x, pltpu.HBM)


def swap(x, bit, count):
    return lax.ppermute(x, "trade", [(i, i ^ (bit | 1)) for i in range(count)])


def join(own, other, bit):
    upper = (lax.axis_index("trade") & bit) != 0
    return jnp.concatenate([jnp.where(upper, other, own), jnp.where(upper, own, other)], axis=0)


def offsets(index, count):
    result = jnp.zeros_like(index)
    bit = 1
    top = count // 2
    while bit < count:
        result = result ^ jnp.where((index & top) != 0, bit | 1, 0)
        bit *= 2
        top //= 2
    return result


def scatter_sums(kept, sent, count):
    bit = 1
    while bit < count // 2:
        x = kept + swap(sent, bit, count)
        half = x.shape[0] // 2
        kept, sent = x[:half], x[half:]
        bit *= 2
    near = sent.shape[1] // 2
    return kept + swap(jnp.concatenate([sent[:, near:], sent[:, :near]], axis=1), bit, count)


def copy_kernel(factors_ref, own_ref):
    own_ref[...] = factors_ref[...]


def rows_kernel(
    count,
    me_ref,
    live_ref,
    limit_hbm,
    loadings_hbm,
    ids_hbm,
    owner_hbm,
    limits_ref,
    split_ref,
    onehot_ref,
    limit_ref,
    loadings_ref,
    ids_ref,
    owner_ref,
    sems,
):
    copies = [
        pltpu.make_async_copy(source, target, sems.at[i])
        for i, (source, target) in enumerate(
            (
                (limit_hbm, limit_ref),
                (loadings_hbm, loadings_ref),
                (ids_hbm, ids_ref),
                (owner_hbm, owner_ref),
            )
        )
    ]
    for copy in copies:
        copy.start()
    for copy in copies:
        copy.wait()
    own_rows = limits_ref.shape[0]
    for r in range(own_rows):
        limits_ref[r : r + 1, :] = jnp.full((1, LANES), limit_ref[r])
    set_total = owner_ref.shape[1]
    place = lax.broadcasted_iota(jnp.int32, (set_total, 1), 0)
    block = lax.shift_right_logical(place, own_rows.bit_length() - 1)
    row_at = (offsets(block, count) ^ me_ref[0]) * own_rows + (place & (own_rows - 1))
    sets = lax.broadcasted_iota(jnp.int32, (set_total, set_total), 1)
    set_at = jnp.sum(jnp.where(row_at == owner_ref[...], sets, 0), axis=1, keepdims=True)
    lane = lax.broadcasted_iota(jnp.int32, (1, LANES), 1)
    live = live_ref[0]
    for c in range(ids_ref.shape[0]):
        ids = jnp.where(lane + c * LANES < live, ids_ref[c : c + 1, :], -1)
        hit = jnp.where(ids == set_at, 1.0, 0.0)
        onehot_ref[:, c * LANES : (c + 1) * LANES] = hit.astype(jnp.bfloat16)
    tall = jnp.concatenate([loadings_ref[...]] * DATES, axis=0)
    wide = jnp.concatenate([tall] * DATES, axis=1)
    row = lax.broadcasted_iota(jnp.int32, wide.shape, 0) // F
    column = lax.broadcasted_iota(jnp.int32, wide.shape, 1) // K
    rest = jnp.where(row == column, wide, 0.0)
    for i in range(3):
        part = rest.astype(jnp.bfloat16)
        split_ref[i] = part
        rest = rest - part.astype(jnp.float32)


def coef_kernel(coef_hbm, size_hbm, used_ref, coef_ref, size_ref, sems):
    parts = sems.shape[0] - 1
    step = coef_ref.shape[0] // parts
    sizes_in = pltpu.make_async_copy(size_hbm, size_ref, sems.at[parts])
    sizes_in.start()
    coef_in = []
    for i in range(parts):
        rows = pl.ds(i * step, step)
        coef_in.append(pltpu.make_async_copy(coef_hbm.at[rows, :], coef_ref.at[rows, :], sems.at[i]))
        coef_in[i].start()
    sizes_in.wait()
    sizes = size_ref[...].astype(jnp.float32).T
    width = coef_ref.shape[1]
    basis = (lax.broadcasted_iota(jnp.int32, (1, width), 1) & (K - 1)).astype(jnp.float32)
    for i in range(parts):
        coef_in[i].wait()
        for c in range(i * step // LANES, (i + 1) * step // LANES):
            rows = slice(c * LANES, (c + 1) * LANES)
            coef = coef_ref[rows, :].astype(jnp.float32)
            used_ref[rows, :] = jnp.where(basis < sizes[:, c : c + 1], coef, 0.0).astype(jnp.bfloat16)


def net_block(paths, split_ref, used_ref, onehot_ref):
    total = paths.shape[0]
    loaded = sum(jnp.dot(paths, split_ref[i], preferred_element_type=jnp.float32) for i in (2, 1, 0))
    tiled = jnp.concatenate([jnp.tanh(loaded)] * DATES, axis=0)
    row = lax.broadcasted_iota(jnp.int32, tiled.shape, 0) // total
    column = lax.broadcasted_iota(jnp.int32, tiled.shape, 1) // K
    table = jnp.where(row == column, tiled, 0.0).astype(jnp.bfloat16)
    slots = used_ref.shape[0]
    step = min(SLOT_BLOCK, slots)
    result = jnp.zeros((onehot_ref.shape[0], DATES * total), jnp.float32)
    for at in range(0, slots, step):
        values = lax.dot_general(
            used_ref[at : at + step, :], table, (((1,), (1,)), ((), ())), preferred_element_type=jnp.float32
        )
        values = values.astype(jnp.bfloat16)
        result = result + jnp.dot(onehot_ref[:, at : at + step], values, preferred_element_type=jnp.float32)
    return result


def near_kernel(paths_ref, split_ref, used_ref, onehot_ref, net_ref):
    block = min(PATH_BLOCK, paths_ref.shape[0])
    for b in range(paths_ref.shape[0] // block):
        net = net_block(paths_ref[b * block : (b + 1) * block, :], split_ref, used_ref, onehot_ref)
        net_ref[:, b * DATES * block : (b + 1) * DATES * block] = net


def far_kernel(paths_ref, split_ref, used_ref, onehot_ref, near_ref, kept_ref, sent_ref):
    half = kept_ref.shape[0]
    width = near_ref.shape[1]
    kept_ref[:, :width] = near_ref[:half, :]
    sent_ref[:, :width] = near_ref[half:, :]
    block = min(PATH_BLOCK, paths_ref.shape[0])
    for b in range(paths_ref.shape[0] // block):
        net = net_block(paths_ref[b * block : (b + 1) * block, :], split_ref, used_ref, onehot_ref)
        at = slice(width + b * DATES * block, width + (b + 1) * DATES * block)
        sent_ref[:, at] = net[half:, :]
        kept_ref[:, at] = net[:half, :]


def body(
    factors,
    loadings,
    trade_coef,
    basis_size,
    set_ids,
    live_count,
    netting_row,
    threshold,
    margin_start,
    *,
    count,
):
    me = lax.axis_index("trade")
    own_rows = threshold.shape[0]
    set_total = netting_row.shape[0]
    slot_total, width = trade_coef.shape
    shape = jax.ShapeDtypeStruct
    f32, bf16 = jnp.float32, jnp.bfloat16

    (own,) = call(copy_kernel, [shape(factors.shape, bf16)], [VMEM], 10**6, (factors,))
    near = join(own, swap(factors, 1, count), 1)
    sizes = basis_size.reshape(-1, LANES)
    sizes, near = lax.optimization_barrier((sizes, near))
    (used,) = call(
        coef_kernel,
        [shape(trade_coef.shape, bf16)],
        [HBM, HBM],
        10**8,
        (in_hbm(trade_coef), in_hbm(sizes)),
        [pltpu.VMEM(trade_coef.shape, bf16), pltpu.VMEM(sizes.shape, jnp.int32), pltpu.SemaphoreType.DMA((PARTS + 1,))],
    )
    near = join(near, swap(near, 2, count), 2)
    ids = set_ids.reshape(-1, LANES)
    owner = netting_row.reshape(1, -1)
    turned = loadings.T
    ids, near = lax.optimization_barrier((ids, near))
    limits, split, onehot = call(
        lambda *refs: rows_kernel(count, *refs),
        [shape((own_rows, LANES), f32), shape((3, DATES * F, DATES * K), bf16), shape((set_total, slot_total), bf16)],
        [SMEM] * 2 + [HBM] * 4,
        10**8,
        (me.astype(jnp.int32).reshape(1), live_count, *map(in_hbm, (threshold, turned, ids, owner))),
        [
            pltpu.SMEM(threshold.shape, f32),
            pltpu.VMEM(turned.shape, f32),
            pltpu.VMEM(ids.shape, jnp.int32),
            pltpu.VMEM(owner.shape, jnp.int32),
            pltpu.SemaphoreType.DMA((4,)),
        ],
    )
    bit = 4
    while bit < count // 2:
        near = join(near, swap(near, bit, count), bit)
        bit *= 2
    far = swap(near, bit, count)
    side_total = near.shape[0]
    columns = DATES * side_total
    work = 2 * columns * slot_total * (width + set_total)
    (near_net,) = call(
        near_kernel, [shape((set_total, columns), f32)], [VMEM] * 4, work, (near, split, used, onehot)
    )
    kept, sent = call(
        far_kernel,
        [shape((set_total // 2, 2 * columns), f32)] * 2,
        [VMEM] * 5,
        work,
        (far, split, used, onehot, near_net),
    )
    netted = scatter_sums(kept, sent, count)

    upper = (me & (count // 2)) != 0
    flipped = jnp.concatenate([margin_start[:, side_total:], margin_start[:, :side_total]], axis=1)
    start = jnp.where(upper, flipped, margin_start)

    block = min(PATH_BLOCK, side_total)
    netted = netted.reshape(own_rows, -1, DATES, block)
    start = start.reshape(own_rows, -1, 1, block)
    margin = jnp.maximum(netted[:, :, : DATES - LAG] - limits[:, :1, None, None], 0.0)
    held = jnp.broadcast_to(start, (own_rows, start.shape[1], LAG, block))
    collateral = jnp.concatenate([held, margin], axis=2)
    shortfall = jnp.sum(jnp.maximum(netted - collateral, 0.0), axis=(1, 3))
    return shortfall / (2 * side_total)


def solution(mesh):
    count = mesh.shape["trade"]

    def local(*args):
        return body(*args, count=count)

    return jax.shard_map(
        local,
        mesh=mesh,
        in_specs=(
            P(("group", "trade"), None),
            P(),
            P(("group", "trade"), None),
            P(("group", "trade")),
            P(("group", "trade")),
            P(("group", "trade")),
            P("group"),
            P(("group", "trade")),
            P(("group", "trade"), None),
        ),
        out_specs=P(("group", "trade"), None),
        check_vma=False,
    )
```

```python
import jax
import jax.numpy as jnp
from jax import lax
from jax.experimental import pallas as pl
from jax.experimental.pallas import tpu as pltpu
from jax.sharding import PartitionSpec as P

F = 16
K = 32
DATES = 8
LAG = 2
LANES = 128
PATH_BLOCK = 32
VMEM = pl.BlockSpec(memory_space=pltpu.VMEM)
SMEM = pl.BlockSpec(memory_space=pltpu.SMEM)
HBM = pl.BlockSpec(memory_space=pltpu.HBM)
PARTS = 4


def call(kernel, outs, specs, flops, args, scratch=()):
    sizes = [a.size * a.dtype.itemsize for a in (*args, *outs)]
    return pl.pallas_call(
        kernel,
        out_shape=outs,
        in_specs=specs,
        out_specs=[VMEM] * len(outs),
        scratch_shapes=scratch,
        compiler_params=pltpu.CompilerParams(vmem_limit_bytes=24 * 2**20),
        cost_estimate=pl.CostEstimate(flops=flops, bytes_accessed=sum(sizes) if flops else 0, transcendentals=0),
    )(*args)


def in_hbm(x):
    return pltpu.with_memory_space_constraint(x, pltpu.HBM)


def swap(x, bit, count):
    return lax.ppermute(x, "trade", [(i, i ^ (bit | 1)) for i in range(count)])


def join(own, other, bit):
    upper = (lax.axis_index("trade") & bit) != 0
    return jnp.concatenate([jnp.where(upper, other, own), jnp.where(upper, own, other)], axis=0)


def rounds(count):
    bits = []
    bit = 2
    while bit < count:
        bits.append(bit)
        bit *= 2
    return bits + [1]


def offsets(index, count):
    result = jnp.zeros_like(index)
    top = count // 2
    for bit in rounds(count):
        result = result ^ jnp.where((index & top) != 0, bit | 1, 0)
        top //= 2
    return result


def parity(index, count):
    result = index & 1
    bit = 2
    while bit < count:
        result = result ^ jnp.where((index & bit) != 0, 1, 0)
        bit *= 2
    return result


def scatter_sums(kept, sent, count):
    near = kept.shape[1] // 2
    for bit in rounds(count)[:-1]:
        if bit == count // 2:
            sent = jnp.concatenate([sent[:, near:], sent[:, :near]], axis=1)
        x = kept + swap(sent, bit, count)
        half = x.shape[0] // 2
        kept, sent = x[:half], x[half:]
    return kept, swap(sent, 1, count)


def fetch_kernel(
    factors_hbm,
    coef_hbm,
    size_hbm,
    ids_hbm,
    owner_hbm,
    margin_hbm,
    limit_hbm,
    loadings_hbm,
    own_ref,
    used_ref,
    ids_ref,
    owner_ref,
    margin_ref,
    limits_ref,
    split_ref,
    coef_ref,
    size_ref,
    limit_ref,
    loadings_ref,
    sems,
):
    slots, width = coef_ref.shape
    step = slots // PARTS
    pairs = (
        (size_hbm, size_ref),
        (limit_hbm, limit_ref),
        (loadings_hbm, loadings_ref),
        (factors_hbm, own_ref),
        (ids_hbm, ids_ref),
        (owner_hbm, owner_ref),
        (margin_hbm, margin_ref),
    )
    small = [pltpu.make_async_copy(source, target, sems.at[PARTS + i]) for i, (source, target) in enumerate(pairs)]
    large = [
        pltpu.make_async_copy(
            coef_hbm.at[pl.ds(i * step, step), :], coef_ref.at[pl.ds(i * step, step), :], sems.at[i]
        )
        for i in range(PARTS)
    ]
    for copy in small[:3] + large + small[3:]:
        copy.start()
    for copy in small[:3]:
        copy.wait()
    for r in range(limits_ref.shape[0]):
        limits_ref[r : r + 1, :] = jnp.full((1, LANES), limit_ref[r])
    tall = jnp.concatenate([loadings_ref[...]] * DATES, axis=0)
    wide = jnp.concatenate([tall] * DATES, axis=1)
    row = lax.broadcasted_iota(jnp.int32, wide.shape, 0) // F
    column = lax.broadcasted_iota(jnp.int32, wide.shape, 1) // K
    rest = jnp.where(row == column, wide, 0.0)
    for i in range(3):
        part = rest.astype(jnp.bfloat16)
        split_ref[i] = part
        rest = rest - part.astype(jnp.float32)
    sizes = size_ref[...].astype(jnp.float32).T
    basis = (lax.broadcasted_iota(jnp.int32, (1, width), 1) & (K - 1)).astype(jnp.float32)
    for i in range(PARTS):
        large[i].wait()
        for c in range(i * step // LANES, (i + 1) * step // LANES):
            rows = slice(c * LANES, (c + 1) * LANES)
            coef = coef_ref[rows, :].astype(jnp.float32)
            used_ref[rows, :] = jnp.where(basis < sizes[:, c : c + 1], coef, 0.0).astype(jnp.bfloat16)
    for copy in small[3:]:
        copy.wait()


def write_onehot(code, set_at, hot_ref):
    for c in range(code.shape[0]):
        hit = jnp.where(code[c : c + 1, :] == set_at, 1.0, 0.0)
        hot_ref[:, c * LANES : (c + 1) * LANES] = hit.astype(jnp.bfloat16)


def rows_kernel(count, own_rows, me_ref, live_ref, ids_ref, owner_ref, set_ref, hot_ref, code_ref):
    set_total = owner_ref.shape[1]
    place = lax.broadcasted_iota(jnp.int32, (set_total, 1), 0)
    block = lax.shift_right_logical(place, own_rows.bit_length() - 1)
    row_at = (offsets(block, count) ^ me_ref[0]) * own_rows + (place & (own_rows - 1))
    sets = lax.broadcasted_iota(jnp.int32, (set_total, set_total), 1)
    set_at = jnp.sum(jnp.where(row_at == owner_ref[...], sets, 0), axis=1, keepdims=True)
    set_ref[...] = jnp.broadcast_to(set_at, set_ref.shape)
    shape = ids_ref.shape
    slot = lax.broadcasted_iota(jnp.int32, shape, 0) * LANES + lax.broadcasted_iota(jnp.int32, shape, 1)
    code = jnp.where(slot < live_ref[0], ids_ref[...], -1)
    code_ref[...] = code
    write_onehot(code, set_at, hot_ref)


def other_rows_kernel(set_ref, code_ref, hot_ref):
    write_onehot(code_ref[...], set_ref[:, :1], hot_ref)


def net_block(paths, split_ref, trades):
    total = paths.shape[0]
    loaded = sum(jnp.dot(paths, split_ref[i], preferred_element_type=jnp.float32) for i in (2, 1, 0))
    tiled = jnp.concatenate([jnp.tanh(loaded)] * DATES, axis=0)
    row = lax.broadcasted_iota(jnp.int32, tiled.shape, 0) // total
    column = lax.broadcasted_iota(jnp.int32, tiled.shape, 1) // K
    table = jnp.where(row == column, tiled, 0.0).astype(jnp.bfloat16)
    result = 0.0
    for used_ref, onehot_ref in trades:
        values = lax.dot_general(
            used_ref[...],
            table,
            (((1,), (1,)), ((), ())),
            preferred_element_type=jnp.float32,
        )
        values = values.astype(jnp.bfloat16)
        result = result + jnp.dot(onehot_ref[...], values, preferred_element_type=jnp.float32)
    return result


def near_kernel(paths_ref, split_ref, used_ref, other_ref, onehot_ref, other_hot_ref, net_ref):
    trades = ((used_ref, onehot_ref), (other_ref, other_hot_ref))
    block = min(PATH_BLOCK, paths_ref.shape[0])
    for b in range(paths_ref.shape[0] // block):
        net = net_block(paths_ref[b * block : (b + 1) * block, :], split_ref, trades)
        net_ref[:, b * DATES * block : (b + 1) * DATES * block] = net


def far_kernel(
    paths_ref, split_ref, used_ref, other_ref, onehot_ref, other_hot_ref, near_ref, kept_ref, sent_ref
):
    half = kept_ref.shape[0]
    width = near_ref.shape[1]
    kept_ref[:, :width] = near_ref[:half, :]
    sent_ref[:, :width] = near_ref[half:, :]
    trades = ((used_ref, onehot_ref), (other_ref, other_hot_ref))
    block = min(PATH_BLOCK, paths_ref.shape[0])
    for b in range(paths_ref.shape[0] // block):
        net = net_block(paths_ref[b * block : (b + 1) * block, :], split_ref, trades)
        at = width + b * DATES * block
        kept_ref[:, at : at + DATES * block] = net[:half, :]
        sent_ref[:, at : at + DATES * block] = net[half:, :]


def body(
    factors,
    loadings,
    trade_coef,
    basis_size,
    set_ids,
    live_count,
    netting_row,
    threshold,
    margin_start,
    *,
    count,
):
    me = lax.axis_index("trade")
    own_rows = threshold.shape[0]
    set_total = netting_row.shape[0]
    slot_total, width = trade_coef.shape
    shape = jax.ShapeDtypeStruct
    f32, bf16 = jnp.float32, jnp.bfloat16

    sizes = basis_size.reshape(-1, LANES)
    ids = set_ids.reshape(-1, LANES)
    owner = netting_row.reshape(1, -1)
    turned = loadings.T
    own, used, ids, owner, margin, limits, split = call(
        fetch_kernel,
        [
            shape(factors.shape, bf16),
            shape(trade_coef.shape, bf16),
            shape(ids.shape, jnp.int32),
            shape(owner.shape, jnp.int32),
            shape(margin_start.shape, f32),
            shape((own_rows, LANES), f32),
            shape((3, DATES * F, DATES * K), bf16),
        ],
        [HBM] * 8,
        10**8,
        tuple(map(in_hbm, (factors, trade_coef, sizes, ids, owner, margin_start, threshold, turned))),
        [
            pltpu.VMEM(trade_coef.shape, bf16),
            pltpu.VMEM(sizes.shape, jnp.int32),
            pltpu.SMEM(threshold.shape, f32),
            pltpu.VMEM(turned.shape, f32),
            pltpu.SemaphoreType.DMA((PARTS + 7,)),
        ],
    )
    near = join(own, swap(factors, 2, count), 2)
    used, ids, live_count, near = lax.optimization_barrier((used, ids, live_count, near))
    other = swap(used, 1, count)
    set_at, onehot, code = call(
        lambda *refs: rows_kernel(count, own_rows, *refs),
        [
            shape((set_total, LANES), jnp.int32),
            shape((set_total, slot_total), bf16),
            shape(ids.shape, jnp.int32),
        ],
        [SMEM] * 2 + [VMEM] * 2,
        0,
        (me.astype(jnp.int32).reshape(1), live_count, ids, owner),
    )
    (other_hot,) = call(
        other_rows_kernel,
        [shape((set_total, slot_total), bf16)],
        [VMEM] * 2,
        10**8,
        (set_at, swap(code, 1, count)),
    )
    bit = 4
    while bit < count // 2:
        near = join(near, swap(near, bit, count), bit)
        bit *= 2
    far = swap(near, bit, count)
    side_total = near.shape[0]
    columns = DATES * side_total
    work = 4 * columns * slot_total * (width + set_total)
    (near_net,) = call(
        near_kernel,
        [shape((set_total, columns), f32)],
        [VMEM] * 6,
        work,
        (near, split, used, other, onehot, other_hot),
    )
    kept, sent = call(
        far_kernel,
        [shape((set_total // 2, 2 * columns), f32)] * 2,
        [VMEM] * 7,
        work,
        (far, split, used, other, onehot, other_hot, near_net),
    )
    margin, limits, me, kept = lax.optimization_barrier((margin, limits, me, kept))
    sums = scatter_sums(kept, sent, count)

    pairs = margin.reshape(own_rows, count // 2, 2, -1)
    odd = parity(2 * jnp.arange(count // 2, dtype=jnp.int32) ^ me, count)[:, None] != 0
    first, second = pairs[:, :, 0], pairs[:, :, 1]
    upper = (me & (count // 2)) != 0
    block = min(PATH_BLOCK, side_total)
    total = 0.0
    for netted, start in zip(sums, (jnp.where(odd, second, first), jnp.where(odd, first, second))):
        start = start.reshape(own_rows, 2, -1)
        start = jnp.where(upper, start[:, ::-1], start).reshape(own_rows, -1, 1, block)
        netted = netted.reshape(own_rows, -1, DATES, block)
        excess = jnp.maximum(netted[:, :, : DATES - LAG] - limits[:, :1, None, None], 0.0)
        held = jnp.broadcast_to(start, (own_rows, start.shape[1], LAG, block))
        collateral = jnp.concatenate([held, excess], axis=2)
        total = total + jnp.sum(jnp.maximum(netted - collateral, 0.0), axis=(1, 3))
    return total / (4 * side_total)


def solution(mesh):
    count = mesh.shape["trade"]

    def local(*args):
        return body(*args, count=count)

    return jax.shard_map(
        local,
        mesh=mesh,
        in_specs=(
            P(("group", "trade"), None),
            P(),
            P(("group", "trade"), None),
            P(("group", "trade")),
            P(("group", "trade")),
            P(("group", "trade")),
            P("group"),
            P(("group", "trade")),
            P(("group", "trade"), None),
        ),
        out_specs=P(("group", "trade"), None),
        check_vma=False,
    )
```

```python
import jax
import jax.numpy as jnp
from jax import lax
from jax.experimental import pallas as pl
from jax.experimental.pallas import tpu as pltpu
from jax.sharding import PartitionSpec as P

F = 16
K = 32
DATES = 8
LAG = 2
LANES = 128
PATH_BLOCK = 32
VMEM = pl.BlockSpec(memory_space=pltpu.VMEM)
SMEM = pl.BlockSpec(memory_space=pltpu.SMEM)
HBM = pl.BlockSpec(memory_space=pltpu.HBM)
PARTS = 4


def call(kernel, outs, specs, flops, args, scratch=()):
    sizes = [a.size * a.dtype.itemsize for a in (*args, *outs)]
    return pl.pallas_call(
        kernel,
        out_shape=outs,
        in_specs=specs,
        out_specs=[VMEM] * len(outs),
        scratch_shapes=scratch,
        compiler_params=pltpu.CompilerParams(vmem_limit_bytes=24 * 2**20),
        cost_estimate=pl.CostEstimate(flops=flops, bytes_accessed=sum(sizes) if flops else 0, transcendentals=0),
    )(*args)


def in_hbm(x):
    return pltpu.with_memory_space_constraint(x, pltpu.HBM)


def swap(x, bit, count):
    return lax.ppermute(x, "trade", [(i, i ^ (bit | 1)) for i in range(count)])


def join(own, other, bit):
    upper = (lax.axis_index("trade") & bit) != 0
    return jnp.concatenate([jnp.where(upper, other, own), jnp.where(upper, own, other)], axis=0)


def rounds(count):
    bits = []
    bit = 2
    while bit < count:
        bits.append(bit)
        bit *= 2
    return bits + [1]


def offsets(index, count):
    result = jnp.zeros_like(index)
    top = count // 2
    for bit in rounds(count):
        result = result ^ jnp.where((index & top) != 0, bit | 1, 0)
        top //= 2
    return result


def parity(index, count):
    result = index & 1
    bit = 2
    while bit < count:
        result = result ^ jnp.where((index & bit) != 0, 1, 0)
        bit *= 2
    return result


def scatter_sums(kept, sent, count):
    near = kept.shape[1] // 2
    for bit in rounds(count)[:-1]:
        if bit == count // 2:
            sent = jnp.concatenate([sent[:, near:], sent[:, :near]], axis=1)
        x = kept + swap(sent, bit, count)
        half = x.shape[0] // 2
        kept, sent = x[:half], x[half:]
    return kept, swap(sent, 1, count)


def fetch_kernel(
    factors_hbm,
    coef_hbm,
    size_hbm,
    ids_hbm,
    owner_hbm,
    margin_hbm,
    limit_hbm,
    loadings_hbm,
    own_ref,
    used_ref,
    ids_ref,
    owner_ref,
    margin_ref,
    limits_ref,
    split_ref,
    coef_ref,
    size_ref,
    limit_ref,
    loadings_ref,
    sems,
):
    slots, width = coef_ref.shape
    step = slots // PARTS
    pairs = (
        (size_hbm, size_ref),
        (limit_hbm, limit_ref),
        (loadings_hbm, loadings_ref),
        (factors_hbm, own_ref),
        (ids_hbm, ids_ref),
        (owner_hbm, owner_ref),
        (margin_hbm, margin_ref),
    )
    small = [pltpu.make_async_copy(source, target, sems.at[PARTS + i]) for i, (source, target) in enumerate(pairs)]
    large = [
        pltpu.make_async_copy(
            coef_hbm.at[pl.ds(i * step, step), :], coef_ref.at[pl.ds(i * step, step), :], sems.at[i]
        )
        for i in range(PARTS)
    ]
    for copy in small[:3] + large + small[3:]:
        copy.start()
    for copy in small[:3]:
        copy.wait()
    for r in range(limits_ref.shape[0]):
        limits_ref[r : r + 1, :] = jnp.full((1, LANES), limit_ref[r])
    tall = jnp.concatenate([loadings_ref[...]] * DATES, axis=0)
    wide = jnp.concatenate([tall] * DATES, axis=1)
    row = lax.broadcasted_iota(jnp.int32, wide.shape, 0) // F
    column = lax.broadcasted_iota(jnp.int32, wide.shape, 1) // K
    rest = jnp.where(row == column, wide, 0.0)
    for i in range(3):
        part = rest.astype(jnp.bfloat16)
        split_ref[i] = part
        rest = rest - part.astype(jnp.float32)
    sizes = size_ref[...].astype(jnp.float32).T
    basis = (lax.broadcasted_iota(jnp.int32, (1, width), 1) & (K - 1)).astype(jnp.float32)
    for i in range(PARTS):
        large[i].wait()
        for c in range(i * step // LANES, (i + 1) * step // LANES):
            rows = slice(c * LANES, (c + 1) * LANES)
            coef = coef_ref[rows, :].astype(jnp.float32)
            used_ref[rows, :] = jnp.where(basis < sizes[:, c : c + 1], coef, 0.0).astype(jnp.bfloat16)
    for copy in small[3:]:
        copy.wait()


def write_onehot(code, set_at, hot_ref):
    for c in range(code.shape[0]):
        hit = jnp.where(code[c : c + 1, :] == set_at, 1.0, 0.0)
        hot_ref[:, c * LANES : (c + 1) * LANES] = hit.astype(jnp.bfloat16)


def held_margin(count, me, margin, held_ref):
    path_total = margin.shape[1]
    own = path_total // count
    side = path_total // 4
    block = min(PATH_BLOCK, side)
    columns = DATES * block
    lane = lax.broadcasted_iota(jnp.int32, (1, columns), 1)
    source = lax.broadcasted_iota(jnp.int32, (path_total, 1), 0)
    mine = parity(me, count)
    far_bit = jnp.where((me & (count // 2)) != 0, 1, 0)
    inner = lane - (lane // block) * block
    at = 0
    for other in range(2):
        for half in range(2):
            for b in range(side // block):
                place = b * block + inner
                device = place // own
                chip = (far_bit ^ half) * (count // 4) + device
                core = parity(chip, count) ^ mine ^ other
                wanted = (2 * chip + core) * own + (place - device * own)
                pick = jnp.where(source == wanted, 1.0, 0.0)
                held_ref[:, at : at + columns] = jnp.dot(
                    margin, pick, precision=lax.Precision.HIGHEST, preferred_element_type=jnp.float32
                )
                at += columns


def final_kernel(own_ref, other_ref, held_ref, limits_ref, out_ref):
    rows, width = own_ref.shape
    side = width // (2 * DATES)
    block = min(PATH_BLOCK, side)
    columns = DATES * block
    limit = jnp.broadcast_to(limits_ref[:, :1], (rows, columns))
    lane = lax.broadcasted_iota(jnp.int32, (rows, columns), 1)
    total = jnp.zeros((rows, columns), jnp.float32)
    at = 0
    for net_ref in (own_ref, other_ref):
        for b in range(width // columns):
            netted = net_ref[:, b * columns : (b + 1) * columns]
            before = pltpu.roll(netted, LAG * block, 1)
            margin = jnp.maximum(before - limit, 0.0)
            collateral = jnp.where(lane < LAG * block, held_ref[:, at : at + columns], margin)
            total = total + jnp.maximum(netted - collateral, 0.0)
            at += columns
    date = lax.broadcasted_iota(jnp.int32, (columns, DATES), 0) // block
    pick = jnp.where(date == lax.broadcasted_iota(jnp.int32, (columns, DATES), 1), 1.0, 0.0)
    out = jnp.dot(total, pick, precision=lax.Precision.HIGHEST, preferred_element_type=jnp.float32)
    out_ref[...] = out / (4 * side)


def rows_kernel(
    count, own_rows, me_ref, live_ref, ids_ref, owner_ref, margin_ref, set_ref, hot_ref, code_ref, held_ref
):
    held_margin(count, me_ref[0], margin_ref[...], held_ref)
    set_total = owner_ref.shape[1]
    place = lax.broadcasted_iota(jnp.int32, (set_total, 1), 0)
    block = lax.shift_right_logical(place, own_rows.bit_length() - 1)
    row_at = (offsets(block, count) ^ me_ref[0]) * own_rows + (place & (own_rows - 1))
    sets = lax.broadcasted_iota(jnp.int32, (set_total, set_total), 1)
    set_at = jnp.sum(jnp.where(row_at == owner_ref[...], sets, 0), axis=1, keepdims=True)
    set_ref[...] = jnp.broadcast_to(set_at, set_ref.shape)
    shape = ids_ref.shape
    slot = lax.broadcasted_iota(jnp.int32, shape, 0) * LANES + lax.broadcasted_iota(jnp.int32, shape, 1)
    code = jnp.where(slot < live_ref[0], ids_ref[...], -1)
    code_ref[...] = code
    write_onehot(code, set_at, hot_ref)


def other_rows_kernel(set_ref, code_ref, hot_ref):
    write_onehot(code_ref[...], set_ref[:, :1], hot_ref)


def net_block(paths, split_ref, trades):
    total = paths.shape[0]
    loaded = sum(jnp.dot(paths, split_ref[i], preferred_element_type=jnp.float32) for i in (2, 1, 0))
    tiled = jnp.concatenate([jnp.tanh(loaded)] * DATES, axis=0)
    row = lax.broadcasted_iota(jnp.int32, tiled.shape, 0) // total
    column = lax.broadcasted_iota(jnp.int32, tiled.shape, 1) // K
    table = jnp.where(row == column, tiled, 0.0).astype(jnp.bfloat16)
    result = 0.0
    for used_ref, onehot_ref in trades:
        values = lax.dot_general(
            used_ref[...],
            table,
            (((1,), (1,)), ((), ())),
            preferred_element_type=jnp.float32,
        )
        values = values.astype(jnp.bfloat16)
        result = result + jnp.dot(onehot_ref[...], values, preferred_element_type=jnp.float32)
    return result


def near_kernel(paths_ref, split_ref, used_ref, other_ref, onehot_ref, other_hot_ref, net_ref):
    trades = ((used_ref, onehot_ref), (other_ref, other_hot_ref))
    block = min(PATH_BLOCK, paths_ref.shape[0])
    for b in range(paths_ref.shape[0] // block):
        net = net_block(paths_ref[b * block : (b + 1) * block, :], split_ref, trades)
        net_ref[:, b * DATES * block : (b + 1) * DATES * block] = net


def far_kernel(
    paths_ref, split_ref, used_ref, other_ref, onehot_ref, other_hot_ref, near_ref, kept_ref, sent_ref
):
    half = kept_ref.shape[0]
    width = near_ref.shape[1]
    kept_ref[:, :width] = near_ref[:half, :]
    sent_ref[:, :width] = near_ref[half:, :]
    trades = ((used_ref, onehot_ref), (other_ref, other_hot_ref))
    block = min(PATH_BLOCK, paths_ref.shape[0])
    for b in range(paths_ref.shape[0] // block):
        net = net_block(paths_ref[b * block : (b + 1) * block, :], split_ref, trades)
        at = width + b * DATES * block
        kept_ref[:, at : at + DATES * block] = net[:half, :]
        sent_ref[:, at : at + DATES * block] = net[half:, :]


def body(
    factors,
    loadings,
    trade_coef,
    basis_size,
    set_ids,
    live_count,
    netting_row,
    threshold,
    margin_start,
    *,
    count,
):
    me = lax.axis_index("trade")
    own_rows = threshold.shape[0]
    set_total = netting_row.shape[0]
    slot_total, width = trade_coef.shape
    shape = jax.ShapeDtypeStruct
    f32, bf16 = jnp.float32, jnp.bfloat16

    sizes = basis_size.reshape(-1, LANES)
    ids = set_ids.reshape(-1, LANES)
    owner = netting_row.reshape(1, -1)
    turned = loadings.T
    own, used, ids, owner, margin, limits, split = call(
        fetch_kernel,
        [
            shape(factors.shape, bf16),
            shape(trade_coef.shape, bf16),
            shape(ids.shape, jnp.int32),
            shape(owner.shape, jnp.int32),
            shape(margin_start.shape, f32),
            shape((own_rows, LANES), f32),
            shape((3, DATES * F, DATES * K), bf16),
        ],
        [HBM] * 8,
        10**8,
        tuple(map(in_hbm, (factors, trade_coef, sizes, ids, owner, margin_start, threshold, turned))),
        [
            pltpu.VMEM(trade_coef.shape, bf16),
            pltpu.VMEM(sizes.shape, jnp.int32),
            pltpu.SMEM(threshold.shape, f32),
            pltpu.VMEM(turned.shape, f32),
            pltpu.SemaphoreType.DMA((PARTS + 7,)),
        ],
    )
    near = join(own, swap(factors, 2, count), 2)
    used, ids, live_count, near = lax.optimization_barrier((used, ids, live_count, near))
    other = swap(used, 1, count)
    set_at, onehot, code, held = call(
        lambda *refs: rows_kernel(count, own_rows, *refs),
        [
            shape((set_total, LANES), jnp.int32),
            shape((set_total, slot_total), bf16),
            shape(ids.shape, jnp.int32),
            shape((own_rows, DATES * margin_start.shape[1]), f32),
        ],
        [SMEM] * 2 + [VMEM] * 3,
        0,
        (me.astype(jnp.int32).reshape(1), live_count, ids, owner, margin),
    )
    (other_hot,) = call(
        other_rows_kernel,
        [shape((set_total, slot_total), bf16)],
        [VMEM] * 2,
        10**8,
        (set_at, swap(code, 1, count)),
    )
    bit = 4
    while bit < count // 2:
        near = join(near, swap(near, bit, count), bit)
        bit *= 2
    far = swap(near, bit, count)
    side_total = near.shape[0]
    columns = DATES * side_total
    work = 4 * columns * slot_total * (width + set_total)
    (near_net,) = call(
        near_kernel,
        [shape((set_total, columns), f32)],
        [VMEM] * 6,
        work,
        (near, split, used, other, onehot, other_hot),
    )
    kept, sent = call(
        far_kernel,
        [shape((set_total // 2, 2 * columns), f32)] * 2,
        [VMEM] * 7,
        work,
        (far, split, used, other, onehot, other_hot, near_net),
    )
    own_net, other_net = scatter_sums(kept, sent, count)
    (expected,) = call(
        final_kernel,
        [shape((own_rows, DATES), f32)],
        [VMEM] * 4,
        10**6,
        (own_net, other_net, held, limits),
    )
    return expected


def solution(mesh):
    count = mesh.shape["trade"]

    def local(*args):
        return body(*args, count=count)

    return jax.shard_map(
        local,
        mesh=mesh,
        in_specs=(
            P(("group", "trade"), None),
            P(),
            P(("group", "trade"), None),
            P(("group", "trade")),
            P(("group", "trade")),
            P(("group", "trade")),
            P("group"),
            P(("group", "trade")),
            P(("group", "trade"), None),
        ),
        out_specs=P(("group", "trade"), None),
        check_vma=False,
    )
```

```python
import jax
import jax.numpy as jnp
from jax import lax
from jax.experimental import pallas as pl
from jax.experimental.pallas import tpu as pltpu
from jax.sharding import PartitionSpec as P

F = 16
K = 32
DATES = 8
LAG = 2
LANES = 128
PATH_BLOCK = 32
VMEM = pl.BlockSpec(memory_space=pltpu.VMEM)
SMEM = pl.BlockSpec(memory_space=pltpu.SMEM)
HBM = pl.BlockSpec(memory_space=pltpu.HBM)
PARTS = 2


def call(kernel, outs, specs, flops, args, scratch=()):
    sizes = [a.size * a.dtype.itemsize for a in (*args, *outs)]
    return pl.pallas_call(
        kernel,
        out_shape=outs,
        in_specs=specs,
        out_specs=[VMEM] * len(outs),
        scratch_shapes=scratch,
        compiler_params=pltpu.CompilerParams(vmem_limit_bytes=24 * 2**20),
        cost_estimate=pl.CostEstimate(flops=flops, bytes_accessed=sum(sizes) if flops else 0, transcendentals=0),
    )(*args)


def in_hbm(x):
    return pltpu.with_memory_space_constraint(x, pltpu.HBM)


def swap(x, bit, count):
    return lax.ppermute(x, "trade", [(i, i ^ (bit | 1)) for i in range(count)])


def join(own, other, bit):
    upper = (lax.axis_index("trade") & bit) != 0
    return jnp.concatenate([jnp.where(upper, other, own), jnp.where(upper, own, other)], axis=0)


def rounds(count):
    bits = []
    bit = 2
    while bit < count:
        bits.append(bit)
        bit *= 2
    return bits + [1]


def offsets(index, count):
    result = jnp.zeros_like(index)
    top = count // 2
    for bit in rounds(count):
        result = result ^ jnp.where((index & top) != 0, bit | 1, 0)
        top //= 2
    return result


def parity(index, count):
    result = index & 1
    bit = 2
    while bit < count:
        result = result ^ jnp.where((index & bit) != 0, 1, 0)
        bit *= 2
    return result


def scatter_sums(kept, sent, count):
    near = kept.shape[1] // 2
    for bit in rounds(count)[:-1]:
        if bit == count // 2:
            sent = jnp.concatenate([sent[:, near:], sent[:, :near]], axis=1)
        x = kept + swap(sent, bit, count)
        half = x.shape[0] // 2
        kept, sent = x[:half], x[half:]
    return kept, swap(sent, 1, count)


def fetch_kernel(
    factors_hbm,
    coef_hbm,
    size_hbm,
    ids_hbm,
    owner_hbm,
    margin_hbm,
    limit_hbm,
    loadings_hbm,
    own_ref,
    used_ref,
    ids_ref,
    owner_ref,
    margin_ref,
    loadings_ref,
    limits_ref,
    coef_ref,
    size_ref,
    limit_ref,
    sems,
):
    slots, width = coef_ref.shape
    step = slots // PARTS
    pairs = (
        (size_hbm, size_ref),
        (limit_hbm, limit_ref),
        (loadings_hbm, loadings_ref),
        (factors_hbm, own_ref),
        (ids_hbm, ids_ref),
        (owner_hbm, owner_ref),
        (margin_hbm, margin_ref),
    )
    small = [pltpu.make_async_copy(source, target, sems.at[PARTS + i]) for i, (source, target) in enumerate(pairs)]
    large = [
        pltpu.make_async_copy(
            coef_hbm.at[pl.ds(i * step, step), :], coef_ref.at[pl.ds(i * step, step), :], sems.at[i]
        )
        for i in range(PARTS)
    ]
    for copy in small[:3] + large + small[3:]:
        copy.start()
    small[0].wait()
    sizes = size_ref[...].astype(jnp.float32).T
    basis = (lax.broadcasted_iota(jnp.int32, (1, width), 1) & (K - 1)).astype(jnp.float32).astype(jnp.bfloat16)
    for i in range(PARTS):
        large[i].wait()
        for c in range(i * step // LANES, (i + 1) * step // LANES):
            rows = slice(c * LANES, (c + 1) * LANES)
            coef = coef_ref[rows, :]
            used_ref[rows, :] = jnp.where(basis < sizes[:, c : c + 1], coef, jnp.zeros_like(coef))
    for copy in small[1:]:
        copy.wait()
    for r in range(limits_ref.shape[0]):
        limits_ref[r : r + 1, :] = jnp.full((1, LANES), limit_ref[r])


def write_onehot(code, set_at, hot_ref):
    for c in range(code.shape[0]):
        hit = jnp.where(code[c : c + 1, :] == set_at, 1.0, 0.0)
        hot_ref[:, c * LANES : (c + 1) * LANES] = hit.astype(jnp.bfloat16)


def held_margin(count, me, margin, held_ref):
    path_total = margin.shape[1]
    own = path_total // count
    side = path_total // 4
    block = min(PATH_BLOCK, side)
    columns = DATES * block
    lane = lax.broadcasted_iota(jnp.int32, (1, columns), 1)
    source = lax.broadcasted_iota(jnp.int32, (path_total, 1), 0)
    mine = parity(me, count)
    far_bit = jnp.where((me & (count // 2)) != 0, 1, 0)
    inner = lane - (lane // block) * block
    at = 0
    for other in range(2):
        for half in range(2):
            for b in range(side // block):
                place = b * block + inner
                device = place // own
                chip = (far_bit ^ half) * (count // 4) + device
                core = parity(chip, count) ^ mine ^ other
                wanted = (2 * chip + core) * own + (place - device * own)
                pick = jnp.where(source == wanted, 1.0, 0.0)
                held_ref[:, at : at + columns] = jnp.dot(
                    margin, pick, precision=lax.Precision.HIGHEST, preferred_element_type=jnp.float32
                )
                at += columns


def final_kernel(own_ref, other_ref, held_ref, limits_ref, out_ref):
    rows, width = own_ref.shape
    side = width // (2 * DATES)
    block = min(PATH_BLOCK, side)
    columns = DATES * block
    limit = jnp.broadcast_to(limits_ref[:, :1], (rows, columns))
    lane = lax.broadcasted_iota(jnp.int32, (rows, columns), 1)
    total = jnp.zeros((rows, columns), jnp.float32)
    at = 0
    for net_ref in (own_ref, other_ref):
        for b in range(width // columns):
            netted = net_ref[:, b * columns : (b + 1) * columns]
            before = pltpu.roll(netted, LAG * block, 1)
            margin = jnp.maximum(before - limit, 0.0)
            collateral = jnp.where(lane < LAG * block, held_ref[:, at : at + columns], margin)
            total = total + jnp.maximum(netted - collateral, 0.0)
            at += columns
    date = lax.broadcasted_iota(jnp.int32, (columns, DATES), 0) // block
    pick = jnp.where(date == lax.broadcasted_iota(jnp.int32, (columns, DATES), 1), 1.0, 0.0)
    out = jnp.dot(total, pick, precision=lax.Precision.HIGHEST, preferred_element_type=jnp.float32)
    out_ref[...] = out / (4 * side)


def rows_kernel(
    count,
    own_rows,
    me_ref,
    live_ref,
    ids_ref,
    owner_ref,
    margin_ref,
    loadings_ref,
    set_ref,
    hot_ref,
    code_ref,
    held_ref,
    split_ref,
):
    held_margin(count, me_ref[0], margin_ref[...], held_ref)
    tall = jnp.concatenate([loadings_ref[...]] * DATES, axis=0)
    wide = jnp.concatenate([tall] * DATES, axis=1)
    row = lax.broadcasted_iota(jnp.int32, wide.shape, 0) // F
    column = lax.broadcasted_iota(jnp.int32, wide.shape, 1) // K
    rest = jnp.where(row == column, wide, 0.0)
    for i in range(3):
        part = rest.astype(jnp.bfloat16)
        split_ref[i] = part
        rest = rest - part.astype(jnp.float32)
    set_total = owner_ref.shape[1]
    place = lax.broadcasted_iota(jnp.int32, (set_total, 1), 0)
    block = lax.shift_right_logical(place, own_rows.bit_length() - 1)
    row_at = (offsets(block, count) ^ me_ref[0]) * own_rows + (place & (own_rows - 1))
    sets = lax.broadcasted_iota(jnp.int32, (set_total, set_total), 1)
    set_at = jnp.sum(jnp.where(row_at == owner_ref[...], sets, 0), axis=1, keepdims=True)
    set_ref[...] = jnp.broadcast_to(set_at, set_ref.shape)
    shape = ids_ref.shape
    slot = lax.broadcasted_iota(jnp.int32, shape, 0) * LANES + lax.broadcasted_iota(jnp.int32, shape, 1)
    code = jnp.where(slot < live_ref[0], ids_ref[...], -1)
    code_ref[...] = code
    write_onehot(code, set_at, hot_ref)


def other_rows_kernel(set_ref, code_ref, hot_ref):
    write_onehot(code_ref[...], set_ref[:, :1], hot_ref)


def net_block(paths, split_ref, trades):
    total = paths.shape[0]
    loaded = sum(jnp.dot(paths, split_ref[i], preferred_element_type=jnp.float32) for i in (2, 1, 0))
    tiled = jnp.concatenate([jnp.tanh(loaded)] * DATES, axis=0)
    row = lax.broadcasted_iota(jnp.int32, tiled.shape, 0) // total
    column = lax.broadcasted_iota(jnp.int32, tiled.shape, 1) // K
    table = jnp.where(row == column, tiled, 0.0).astype(jnp.bfloat16)
    result = 0.0
    for used_ref, onehot_ref in trades:
        values = lax.dot_general(
            used_ref[...],
            table,
            (((1,), (1,)), ((), ())),
            preferred_element_type=jnp.float32,
        )
        values = values.astype(jnp.bfloat16)
        result = result + jnp.dot(onehot_ref[...], values, preferred_element_type=jnp.float32)
    return result


def near_kernel(paths_ref, split_ref, used_ref, other_ref, onehot_ref, other_hot_ref, net_ref):
    trades = ((used_ref, onehot_ref), (other_ref, other_hot_ref))
    block = min(PATH_BLOCK, paths_ref.shape[0])
    for b in range(paths_ref.shape[0] // block):
        net = net_block(paths_ref[b * block : (b + 1) * block, :], split_ref, trades)
        net_ref[:, b * DATES * block : (b + 1) * DATES * block] = net


def far_kernel(
    paths_ref, split_ref, used_ref, other_ref, onehot_ref, other_hot_ref, near_ref, kept_ref, sent_ref
):
    half = kept_ref.shape[0]
    width = near_ref.shape[1]
    kept_ref[:, :width] = near_ref[:half, :]
    sent_ref[:, :width] = near_ref[half:, :]
    trades = ((used_ref, onehot_ref), (other_ref, other_hot_ref))
    block = min(PATH_BLOCK, paths_ref.shape[0])
    for b in range(paths_ref.shape[0] // block):
        net = net_block(paths_ref[b * block : (b + 1) * block, :], split_ref, trades)
        at = width + b * DATES * block
        kept_ref[:, at : at + DATES * block] = net[:half, :]
        sent_ref[:, at : at + DATES * block] = net[half:, :]


def body(
    factors,
    loadings,
    trade_coef,
    basis_size,
    set_ids,
    live_count,
    netting_row,
    threshold,
    margin_start,
    *,
    count,
):
    me = lax.axis_index("trade")
    own_rows = threshold.shape[0]
    set_total = netting_row.shape[0]
    slot_total, width = trade_coef.shape
    shape = jax.ShapeDtypeStruct
    f32, bf16 = jnp.float32, jnp.bfloat16

    sizes = basis_size.reshape(-1, LANES)
    ids = set_ids.reshape(-1, LANES)
    owner = netting_row.reshape(1, -1)
    turned = loadings.T
    own, used, ids, owner, margin, turned, limits = call(
        fetch_kernel,
        [
            shape(factors.shape, bf16),
            shape(trade_coef.shape, bf16),
            shape(ids.shape, jnp.int32),
            shape(owner.shape, jnp.int32),
            shape(margin_start.shape, f32),
            shape(turned.shape, f32),
            shape((own_rows, LANES), f32),
        ],
        [HBM] * 8,
        10**8,
        tuple(map(in_hbm, (factors, trade_coef, sizes, ids, owner, margin_start, threshold, turned))),
        [
            pltpu.VMEM(trade_coef.shape, bf16),
            pltpu.VMEM(sizes.shape, jnp.int32),
            pltpu.SMEM(threshold.shape, f32),
            pltpu.SemaphoreType.DMA((PARTS + 7,)),
        ],
    )
    near = join(own, swap(factors, 2, count), 2)
    used, ids, live_count, near = lax.optimization_barrier((used, ids, live_count, near))
    other = swap(used, 1, count)
    set_at, onehot, code, held, split = call(
        lambda *refs: rows_kernel(count, own_rows, *refs),
        [
            shape((set_total, LANES), jnp.int32),
            shape((set_total, slot_total), bf16),
            shape(ids.shape, jnp.int32),
            shape((own_rows, DATES * margin_start.shape[1]), f32),
            shape((3, DATES * F, DATES * K), bf16),
        ],
        [SMEM] * 2 + [VMEM] * 4,
        0,
        (me.astype(jnp.int32).reshape(1), live_count, ids, owner, margin, turned),
    )
    (other_hot,) = call(
        other_rows_kernel,
        [shape((set_total, slot_total), bf16)],
        [VMEM] * 2,
        10**8,
        (set_at, swap(code, 1, count)),
    )
    bit = 4
    while bit < count // 2:
        near = join(near, swap(near, bit, count), bit)
        bit *= 2
    far = swap(near, bit, count)
    side_total = near.shape[0]
    columns = DATES * side_total
    work = 4 * columns * slot_total * (width + set_total)
    (near_net,) = call(
        near_kernel,
        [shape((set_total, columns), f32)],
        [VMEM] * 6,
        work,
        (near, split, used, other, onehot, other_hot),
    )
    kept, sent = call(
        far_kernel,
        [shape((set_total // 2, 2 * columns), f32)] * 2,
        [VMEM] * 7,
        work,
        (far, split, used, other, onehot, other_hot, near_net),
    )
    own_net, other_net = scatter_sums(kept, sent, count)
    (expected,) = call(
        final_kernel,
        [shape((own_rows, DATES), f32)],
        [VMEM] * 4,
        10**6,
        (own_net, other_net, held, limits),
    )
    return expected


def solution(mesh):
    count = mesh.shape["trade"]

    def local(*args):
        return body(*args, count=count)

    return jax.shard_map(
        local,
        mesh=mesh,
        in_specs=(
            P(("group", "trade"), None),
            P(),
            P(("group", "trade"), None),
            P(("group", "trade")),
            P(("group", "trade")),
            P(("group", "trade")),
            P("group"),
            P(("group", "trade")),
            P(("group", "trade"), None),
        ),
        out_specs=P(("group", "trade"), None),
        check_vma=False,
    )
```

```python
import jax
import jax.numpy as jnp
from jax import lax
from jax.experimental import pallas as pl
from jax.experimental.pallas import tpu as pltpu
from jax.sharding import PartitionSpec as P

F = 16
K = 32
DATES = 8
LAG = 2
LANES = 128
PATH_BLOCK = 32
VMEM = pl.BlockSpec(memory_space=pltpu.VMEM)
SMEM = pl.BlockSpec(memory_space=pltpu.SMEM)
HBM = pl.BlockSpec(memory_space=pltpu.HBM)
PARTS = 2


def call(kernel, outs, specs, flops, args, scratch=()):
    sizes = [a.size * a.dtype.itemsize for a in (*args, *outs)]
    return pl.pallas_call(
        kernel,
        out_shape=outs,
        in_specs=specs,
        out_specs=[VMEM] * len(outs),
        scratch_shapes=scratch,
        compiler_params=pltpu.CompilerParams(vmem_limit_bytes=24 * 2**20),
        cost_estimate=pl.CostEstimate(flops=flops, bytes_accessed=sum(sizes) if flops else 0, transcendentals=0),
    )(*args)


def in_hbm(x):
    return pltpu.with_memory_space_constraint(x, pltpu.HBM)


def swap(x, bit, count):
    return lax.ppermute(x, "trade", [(i, i ^ (bit | 1)) for i in range(count)])


def join(own, other, bit):
    upper = (lax.axis_index("trade") & bit) != 0
    return jnp.concatenate([jnp.where(upper, other, own), jnp.where(upper, own, other)], axis=0)


def rounds(count):
    bits = []
    bit = 2
    while bit < count:
        bits.append(bit)
        bit *= 2
    return bits + [1]


def offsets(index, count):
    result = jnp.zeros_like(index)
    top = count // 2
    for bit in rounds(count):
        result = result ^ jnp.where((index & top) != 0, bit | 1, 0)
        top //= 2
    return result


def parity(index, count):
    result = index & 1
    bit = 2
    while bit < count:
        result = result ^ jnp.where((index & bit) != 0, 1, 0)
        bit *= 2
    return result


def scatter_sums(kept, sent, count):
    near = kept.shape[1] // 2
    for bit in rounds(count)[:-1]:
        if bit == count // 2:
            sent = jnp.concatenate([sent[:, near:], sent[:, :near]], axis=1)
        x = kept + swap(sent, bit, count)
        half = x.shape[0] // 2
        kept, sent = x[:half], x[half:]
    return kept, swap(sent, 1, count)


def fetch_kernel(
    factors_hbm,
    coef_hbm,
    size_hbm,
    ids_hbm,
    owner_hbm,
    margin_hbm,
    limit_hbm,
    loadings_hbm,
    own_ref,
    used_ref,
    ids_ref,
    owner_ref,
    margin_ref,
    loadings_ref,
    limits_ref,
    coef_ref,
    size_ref,
    limit_ref,
    sems,
):
    slots, width = coef_ref.shape
    step = slots // PARTS
    pairs = (
        (size_hbm, size_ref),
        (limit_hbm, limit_ref),
        (loadings_hbm, loadings_ref),
        (factors_hbm, own_ref),
        (ids_hbm, ids_ref),
        (owner_hbm, owner_ref),
        (margin_hbm, margin_ref),
    )
    small = [pltpu.make_async_copy(source, target, sems.at[PARTS + i]) for i, (source, target) in enumerate(pairs)]
    large = [
        pltpu.make_async_copy(
            coef_hbm.at[pl.ds(i * step, step), :], coef_ref.at[pl.ds(i * step, step), :], sems.at[i]
        )
        for i in range(PARTS)
    ]
    for copy in small[:3] + large + small[3:]:
        copy.start()
    small[0].wait()
    sizes = size_ref[...].astype(jnp.float32).T
    basis = (lax.broadcasted_iota(jnp.int32, (1, width), 1) & (K - 1)).astype(jnp.float32).astype(jnp.bfloat16)
    for i in range(PARTS):
        large[i].wait()
        for c in range(i * step // LANES, (i + 1) * step // LANES):
            rows = slice(c * LANES, (c + 1) * LANES)
            coef = coef_ref[rows, :]
            used_ref[rows, :] = jnp.where(basis < sizes[:, c : c + 1], coef, jnp.zeros_like(coef))
    for copy in small[1:]:
        copy.wait()
    for r in range(limits_ref.shape[0]):
        limits_ref[r : r + 1, :] = jnp.full((1, LANES), limit_ref[r])


def write_onehot(code, set_at, hot_ref):
    for c in range(code.shape[0]):
        hit = jnp.where(code[c : c + 1, :] == set_at, 1.0, 0.0)
        hot_ref[:, c * LANES : (c + 1) * LANES] = hit.astype(jnp.bfloat16)


def held_margin(count, me, margin, held_ref):
    path_total = margin.shape[1]
    own = path_total // count
    side = path_total // 4
    block = min(PATH_BLOCK, side)
    columns = DATES * block
    lane = lax.broadcasted_iota(jnp.int32, (1, columns), 1)
    source = lax.broadcasted_iota(jnp.int32, (path_total, 1), 0)
    mine = parity(me, count)
    far_bit = jnp.where((me & (count // 2)) != 0, 1, 0)
    inner = lane - (lane // block) * block
    at = 0
    for other in range(2):
        for half in range(2):
            for b in range(side // block):
                place = b * block + inner
                device = place // own
                chip = (far_bit ^ half) * (count // 4) + device
                core = parity(chip, count) ^ mine ^ other
                wanted = (2 * chip + core) * own + (place - device * own)
                pick = jnp.where(source == wanted, 1.0, 0.0)
                held_ref[:, at : at + columns] = jnp.dot(
                    margin, pick, precision=lax.Precision.HIGHEST, preferred_element_type=jnp.float32
                )
                at += columns


def shortfall(net_ref, held_ref, limits_ref, at):
    rows, width = net_ref.shape
    block = min(PATH_BLOCK, width // (2 * DATES))
    columns = DATES * block
    limit = jnp.broadcast_to(limits_ref[:, :1], (rows, columns))
    lane = lax.broadcasted_iota(jnp.int32, (rows, columns), 1)
    total = jnp.zeros((rows, columns), jnp.float32)
    for b in range(width // columns):
        netted = net_ref[:, b * columns : (b + 1) * columns]
        margin = jnp.maximum(pltpu.roll(netted, LAG * block, 1) - limit, 0.0)
        held = held_ref[:, at + b * columns : at + (b + 1) * columns]
        collateral = jnp.where(lane < LAG * block, held, margin)
        total = total + jnp.maximum(netted - collateral, 0.0)
    return total


def own_kernel(own_ref, held_ref, limits_ref, total_ref):
    total_ref[...] = shortfall(own_ref, held_ref, limits_ref, 0)


def final_kernel(other_ref, held_ref, limits_ref, own_ref, out_ref):
    rows, width = other_ref.shape
    columns = own_ref.shape[1]
    rest = own_ref[...] + shortfall(other_ref, held_ref, limits_ref, width)
    date = lax.broadcasted_iota(jnp.int32, (columns, DATES), 0) // (columns // DATES)
    pick = jnp.where(date == lax.broadcasted_iota(jnp.int32, (columns, DATES), 1), 1.0, 0.0).astype(jnp.bfloat16)
    out = jnp.zeros((rows, DATES), jnp.float32)
    for _ in range(3):
        part = rest.astype(jnp.bfloat16)
        out = out + jnp.dot(part, pick, preferred_element_type=jnp.float32)
        rest = rest - part.astype(jnp.float32)
    out_ref[...] = out / (2 * width // DATES)


def rows_kernel(
    count,
    own_rows,
    me_ref,
    live_ref,
    ids_ref,
    owner_ref,
    margin_ref,
    loadings_ref,
    set_ref,
    hot_ref,
    code_ref,
    held_ref,
    split_ref,
):
    held_margin(count, me_ref[0], margin_ref[...], held_ref)
    tall = jnp.concatenate([loadings_ref[...]] * DATES, axis=0)
    wide = jnp.concatenate([tall] * DATES, axis=1)
    row = lax.broadcasted_iota(jnp.int32, wide.shape, 0) // F
    column = lax.broadcasted_iota(jnp.int32, wide.shape, 1) // K
    rest = jnp.where(row == column, wide, 0.0)
    for i in range(3):
        part = rest.astype(jnp.bfloat16)
        split_ref[i] = part
        rest = rest - part.astype(jnp.float32)
    set_total = owner_ref.shape[1]
    place = lax.broadcasted_iota(jnp.int32, (set_total, 1), 0)
    block = lax.shift_right_logical(place, own_rows.bit_length() - 1)
    row_at = (offsets(block, count) ^ me_ref[0]) * own_rows + (place & (own_rows - 1))
    sets = lax.broadcasted_iota(jnp.int32, (set_total, set_total), 1)
    set_at = jnp.sum(jnp.where(row_at == owner_ref[...], sets, 0), axis=1, keepdims=True)
    set_ref[...] = jnp.broadcast_to(set_at, set_ref.shape)
    shape = ids_ref.shape
    slot = lax.broadcasted_iota(jnp.int32, shape, 0) * LANES + lax.broadcasted_iota(jnp.int32, shape, 1)
    code = jnp.where(slot < live_ref[0], ids_ref[...], -1)
    code_ref[...] = code
    write_onehot(code, set_at, hot_ref)


def other_rows_kernel(set_ref, code_ref, hot_ref):
    write_onehot(code_ref[...], set_ref[:, :1], hot_ref)


def net_block(paths, split_ref, trades):
    total = paths.shape[0]
    loaded = sum(jnp.dot(paths, split_ref[i], preferred_element_type=jnp.float32) for i in (2, 1, 0))
    tiled = jnp.concatenate([jnp.tanh(loaded)] * DATES, axis=0)
    row = lax.broadcasted_iota(jnp.int32, tiled.shape, 0) // total
    column = lax.broadcasted_iota(jnp.int32, tiled.shape, 1) // K
    table = jnp.where(row == column, tiled, 0.0).astype(jnp.bfloat16)
    result = 0.0
    for used_ref, onehot_ref in trades:
        values = lax.dot_general(
            used_ref[...],
            table,
            (((1,), (1,)), ((), ())),
            preferred_element_type=jnp.float32,
        )
        values = values.astype(jnp.bfloat16)
        result = result + jnp.dot(onehot_ref[...], values, preferred_element_type=jnp.float32)
    return result


def near_kernel(paths_ref, split_ref, used_ref, other_ref, onehot_ref, other_hot_ref, net_ref):
    trades = ((used_ref, onehot_ref), (other_ref, other_hot_ref))
    block = min(PATH_BLOCK, paths_ref.shape[0])
    for b in range(paths_ref.shape[0] // block):
        net = net_block(paths_ref[b * block : (b + 1) * block, :], split_ref, trades)
        net_ref[:, b * DATES * block : (b + 1) * DATES * block] = net


def far_kernel(
    paths_ref, split_ref, used_ref, other_ref, onehot_ref, other_hot_ref, near_ref, kept_ref, sent_ref
):
    half = kept_ref.shape[0]
    width = near_ref.shape[1]
    kept_ref[:, :width] = near_ref[:half, :]
    sent_ref[:, :width] = near_ref[half:, :]
    trades = ((used_ref, onehot_ref), (other_ref, other_hot_ref))
    block = min(PATH_BLOCK, paths_ref.shape[0])
    for b in range(paths_ref.shape[0] // block):
        net = net_block(paths_ref[b * block : (b + 1) * block, :], split_ref, trades)
        at = width + b * DATES * block
        kept_ref[:, at : at + DATES * block] = net[:half, :]
        sent_ref[:, at : at + DATES * block] = net[half:, :]


def body(
    factors,
    loadings,
    trade_coef,
    basis_size,
    set_ids,
    live_count,
    netting_row,
    threshold,
    margin_start,
    *,
    count,
):
    me = lax.axis_index("trade")
    own_rows = threshold.shape[0]
    set_total = netting_row.shape[0]
    slot_total, width = trade_coef.shape
    shape = jax.ShapeDtypeStruct
    f32, bf16 = jnp.float32, jnp.bfloat16

    sizes = basis_size.reshape(-1, LANES)
    ids = set_ids.reshape(-1, LANES)
    owner = netting_row.reshape(1, -1)
    turned = loadings.T
    own, used, ids, owner, margin, turned, limits = call(
        fetch_kernel,
        [
            shape(factors.shape, bf16),
            shape(trade_coef.shape, bf16),
            shape(ids.shape, jnp.int32),
            shape(owner.shape, jnp.int32),
            shape(margin_start.shape, f32),
            shape(turned.shape, f32),
            shape((own_rows, LANES), f32),
        ],
        [HBM] * 8,
        10**8,
        tuple(map(in_hbm, (factors, trade_coef, sizes, ids, owner, margin_start, threshold, turned))),
        [
            pltpu.VMEM(trade_coef.shape, bf16),
            pltpu.VMEM(sizes.shape, jnp.int32),
            pltpu.SMEM(threshold.shape, f32),
            pltpu.SemaphoreType.DMA((PARTS + 7,)),
        ],
    )
    near = join(own, swap(factors, 2, count), 2)
    used, ids, live_count, near = lax.optimization_barrier((used, ids, live_count, near))
    other = swap(used, 1, count)
    set_at, onehot, code, held, split = call(
        lambda *refs: rows_kernel(count, own_rows, *refs),
        [
            shape((set_total, LANES), jnp.int32),
            shape((set_total, slot_total), bf16),
            shape(ids.shape, jnp.int32),
            shape((own_rows, DATES * margin_start.shape[1]), f32),
            shape((3, DATES * F, DATES * K), bf16),
        ],
        [SMEM] * 2 + [VMEM] * 4,
        0,
        (me.astype(jnp.int32).reshape(1), live_count, ids, owner, margin, turned),
    )
    (other_hot,) = call(
        other_rows_kernel,
        [shape((set_total, slot_total), bf16)],
        [VMEM] * 2,
        10**8,
        (set_at, swap(code, 1, count)),
    )
    bit = 4
    while bit < count // 2:
        near = join(near, swap(near, bit, count), bit)
        bit *= 2
    far = swap(near, bit, count)
    side_total = near.shape[0]
    columns = DATES * side_total
    work = 4 * columns * slot_total * (width + set_total)
    (near_net,) = call(
        near_kernel,
        [shape((set_total, columns), f32)],
        [VMEM] * 6,
        work,
        (near, split, used, other, onehot, other_hot),
    )
    kept, sent = call(
        far_kernel,
        [shape((set_total // 2, 2 * columns), f32)] * 2,
        [VMEM] * 7,
        work,
        (far, split, used, other, onehot, other_hot, near_net),
    )
    own_net, other_net = scatter_sums(kept, sent, count)
    (own_total,) = call(
        own_kernel,
        [shape((own_rows, DATES * min(PATH_BLOCK, side_total)), f32)],
        [VMEM] * 3,
        10**6,
        (own_net, held, limits),
    )
    (expected,) = call(
        final_kernel,
        [shape((own_rows, DATES), f32)],
        [VMEM] * 4,
        10**6,
        (other_net, held, limits, own_total),
    )
    return expected


def solution(mesh):
    count = mesh.shape["trade"]

    def local(*args):
        return body(*args, count=count)

    return jax.shard_map(
        local,
        mesh=mesh,
        in_specs=(
            P(("group", "trade"), None),
            P(),
            P(("group", "trade"), None),
            P(("group", "trade")),
            P(("group", "trade")),
            P(("group", "trade")),
            P("group"),
            P(("group", "trade")),
            P(("group", "trade"), None),
        ),
        out_specs=P(("group", "trade"), None),
        check_vma=False,
    )
```

```python
import jax
import jax.numpy as jnp
from jax import lax
from jax.experimental import pallas as pl
from jax.experimental.pallas import tpu as pltpu
from jax.sharding import PartitionSpec as P

F = 16
K = 32
DATES = 8
LAG = 2
LANES = 128
PATH_BLOCK = 32
SLOT_BLOCK = 1024
VMEM = pl.BlockSpec(memory_space=pltpu.VMEM)
SMEM = pl.BlockSpec(memory_space=pltpu.SMEM)
HBM = pl.BlockSpec(memory_space=pltpu.HBM)
PARTS = 2


def call(kernel, outs, specs, flops, args, scratch=()):
    sizes = [a.size * a.dtype.itemsize for a in (*args, *outs)]
    return pl.pallas_call(
        kernel,
        out_shape=outs,
        in_specs=specs,
        out_specs=[VMEM] * len(outs),
        scratch_shapes=scratch,
        compiler_params=pltpu.CompilerParams(vmem_limit_bytes=24 * 2**20),
        cost_estimate=pl.CostEstimate(flops=flops, bytes_accessed=sum(sizes) if flops else 0, transcendentals=0),
    )(*args)


def in_hbm(x):
    return pltpu.with_memory_space_constraint(x, pltpu.HBM)


def swap(x, bit, count):
    return lax.ppermute(x, "trade", [(i, i ^ (bit | 1)) for i in range(count)])


def join(own, other, bit):
    upper = (lax.axis_index("trade") & bit) != 0
    return jnp.concatenate([jnp.where(upper, other, own), jnp.where(upper, own, other)], axis=0)


def rounds(count):
    bits = []
    bit = 2
    while bit < count:
        bits.append(bit)
        bit *= 2
    return bits + [1]


def offsets(index, count):
    result = jnp.zeros_like(index)
    top = count // 2
    for bit in rounds(count):
        result = result ^ jnp.where((index & top) != 0, bit | 1, 0)
        top //= 2
    return result


def parity(index, count):
    result = index & 1
    bit = 2
    while bit < count:
        result = result ^ jnp.where((index & bit) != 0, 1, 0)
        bit *= 2
    return result


def scatter_sums(kept, sent, count):
    near = kept.shape[1] // 2
    for bit in rounds(count)[:-1]:
        if bit == count // 2:
            sent = jnp.concatenate([sent[:, near:], sent[:, :near]], axis=1)
        x = kept + swap(sent, bit, count)
        half = x.shape[0] // 2
        kept, sent = x[:half], x[half:]
    return kept, swap(sent, 1, count)


def fetch_kernel(
    factors_hbm,
    coef_hbm,
    size_hbm,
    ids_hbm,
    owner_hbm,
    margin_hbm,
    limit_hbm,
    loadings_hbm,
    own_ref,
    used_ref,
    ids_ref,
    owner_ref,
    margin_ref,
    loadings_ref,
    limits_ref,
    coef_ref,
    size_ref,
    limit_ref,
    sems,
):
    slots, width = coef_ref.shape
    step = slots // PARTS
    pairs = (
        (size_hbm, size_ref),
        (limit_hbm, limit_ref),
        (loadings_hbm, loadings_ref),
        (factors_hbm, own_ref),
        (ids_hbm, ids_ref),
        (owner_hbm, owner_ref),
        (margin_hbm, margin_ref),
    )
    small = [pltpu.make_async_copy(source, target, sems.at[PARTS + i]) for i, (source, target) in enumerate(pairs)]
    large = [
        pltpu.make_async_copy(
            coef_hbm.at[pl.ds(i * step, step), :], coef_ref.at[pl.ds(i * step, step), :], sems.at[i]
        )
        for i in range(PARTS)
    ]
    for copy in small[:3] + large + small[3:]:
        copy.start()
    small[0].wait()
    sizes = size_ref[...].astype(jnp.float32).T
    basis = (lax.broadcasted_iota(jnp.int32, (1, width), 1) & (K - 1)).astype(jnp.float32).astype(jnp.bfloat16)
    for i in range(PARTS):
        large[i].wait()
        for c in range(i * step // LANES, (i + 1) * step // LANES):
            rows = slice(c * LANES, (c + 1) * LANES)
            coef = coef_ref[rows, :]
            used_ref[rows, :] = jnp.where(basis < sizes[:, c : c + 1], coef, jnp.zeros_like(coef))
    for copy in small[1:]:
        copy.wait()
    for r in range(limits_ref.shape[0]):
        limits_ref[r : r + 1, :] = jnp.full((1, LANES), limit_ref[r])


def write_onehot(code, set_at, hot_ref):
    for c in range(code.shape[0]):
        hit = jnp.where(code[c : c + 1, :] == set_at, 1.0, 0.0)
        hot_ref[:, c * LANES : (c + 1) * LANES] = hit.astype(jnp.bfloat16)


def held_margin(count, me, margin, held_ref):
    path_total = margin.shape[1]
    own = path_total // count
    side = path_total // 4
    block = min(PATH_BLOCK, side)
    columns = DATES * block
    lane = lax.broadcasted_iota(jnp.int32, (1, columns), 1)
    source = lax.broadcasted_iota(jnp.int32, (path_total, 1), 0)
    mine = parity(me, count)
    far_bit = jnp.where((me & (count // 2)) != 0, 1, 0)
    inner = lane - (lane // block) * block
    at = 0
    for other in range(2):
        for half in range(2):
            for b in range(side // block):
                place = b * block + inner
                device = place // own
                chip = (far_bit ^ half) * (count // 4) + device
                core = parity(chip, count) ^ mine ^ other
                wanted = (2 * chip + core) * own + (place - device * own)
                pick = jnp.where(source == wanted, 1.0, 0.0)
                held_ref[:, at : at + columns] = jnp.dot(
                    margin, pick, precision=lax.Precision.HIGHEST, preferred_element_type=jnp.float32
                )
                at += columns


def shortfall(net_ref, held_ref, limits_ref, at):
    rows, width = net_ref.shape
    block = min(PATH_BLOCK, width // (2 * DATES))
    columns = DATES * block
    limit = jnp.broadcast_to(limits_ref[:, :1], (rows, columns))
    lane = lax.broadcasted_iota(jnp.int32, (rows, columns), 1)
    total = jnp.zeros((rows, columns), jnp.float32)
    for b in range(width // columns):
        netted = net_ref[:, b * columns : (b + 1) * columns]
        margin = jnp.maximum(pltpu.roll(netted, LAG * block, 1) - limit, 0.0)
        held = held_ref[:, at + b * columns : at + (b + 1) * columns]
        collateral = jnp.where(lane < LAG * block, held, margin)
        total = total + jnp.maximum(netted - collateral, 0.0)
    return total


def own_kernel(own_ref, held_ref, limits_ref, total_ref):
    total_ref[...] = shortfall(own_ref, held_ref, limits_ref, 0)


def final_kernel(other_ref, held_ref, limits_ref, own_ref, out_ref):
    rows, width = other_ref.shape
    columns = own_ref.shape[1]
    rest = own_ref[...] + shortfall(other_ref, held_ref, limits_ref, width)
    date = lax.broadcasted_iota(jnp.int32, (columns, DATES), 0) // (columns // DATES)
    pick = jnp.where(date == lax.broadcasted_iota(jnp.int32, (columns, DATES), 1), 1.0, 0.0).astype(jnp.bfloat16)
    out = jnp.zeros((rows, DATES), jnp.float32)
    for _ in range(3):
        part = rest.astype(jnp.bfloat16)
        out = out + jnp.dot(part, pick, preferred_element_type=jnp.float32)
        rest = rest - part.astype(jnp.float32)
    out_ref[...] = out / (2 * width // DATES)


def rows_kernel(
    count,
    own_rows,
    me_ref,
    live_ref,
    ids_ref,
    owner_ref,
    margin_ref,
    loadings_ref,
    set_ref,
    hot_ref,
    code_ref,
    held_ref,
    split_ref,
):
    held_margin(count, me_ref[0], margin_ref[...], held_ref)
    tall = jnp.concatenate([loadings_ref[...]] * DATES, axis=0)
    wide = jnp.concatenate([tall] * DATES, axis=1)
    row = lax.broadcasted_iota(jnp.int32, wide.shape, 0) // F
    column = lax.broadcasted_iota(jnp.int32, wide.shape, 1) // K
    rest = jnp.where(row == column, wide, 0.0)
    for i in range(3):
        part = rest.astype(jnp.bfloat16)
        split_ref[i] = part
        rest = rest - part.astype(jnp.float32)
    set_total = owner_ref.shape[1]
    place = lax.broadcasted_iota(jnp.int32, (set_total, 1), 0)
    block = lax.shift_right_logical(place, own_rows.bit_length() - 1)
    row_at = (offsets(block, count) ^ me_ref[0]) * own_rows + (place & (own_rows - 1))
    sets = lax.broadcasted_iota(jnp.int32, (set_total, set_total), 1)
    set_at = jnp.sum(jnp.where(row_at == owner_ref[...], sets, 0), axis=1, keepdims=True)
    set_ref[...] = jnp.broadcast_to(set_at, set_ref.shape)
    shape = ids_ref.shape
    slot = lax.broadcasted_iota(jnp.int32, shape, 0) * LANES + lax.broadcasted_iota(jnp.int32, shape, 1)
    code = jnp.where(slot < live_ref[0], ids_ref[...], -1)
    code_ref[...] = code
    write_onehot(code, set_at, hot_ref)


def other_rows_kernel(set_ref, code_ref, hot_ref):
    write_onehot(code_ref[...], set_ref[:, :1], hot_ref)


def net_block(paths, split_ref, trades):
    total = paths.shape[0]
    loaded = sum(jnp.dot(paths, split_ref[i], preferred_element_type=jnp.float32) for i in (2, 1, 0))
    tiled = jnp.concatenate([jnp.tanh(loaded)] * DATES, axis=0)
    row = lax.broadcasted_iota(jnp.int32, tiled.shape, 0) // total
    column = lax.broadcasted_iota(jnp.int32, tiled.shape, 1) // K
    table = jnp.where(row == column, tiled, 0.0).astype(jnp.bfloat16)
    result = 0.0
    for used_ref, onehot_ref in trades:
        slots = used_ref.shape[0]
        step = min(SLOT_BLOCK, slots)
        values = [
            lax.dot_general(
                used_ref[at : at + step, :], table, (((1,), (1,)), ((), ())), preferred_element_type=jnp.float32
            ).astype(jnp.bfloat16)
            for at in range(0, slots, step)
        ]
        values = jnp.concatenate(values, axis=0)
        result = result + jnp.dot(onehot_ref[...], values, preferred_element_type=jnp.float32)
    return result


def near_kernel(paths_ref, split_ref, used_ref, other_ref, onehot_ref, other_hot_ref, net_ref):
    trades = ((used_ref, onehot_ref), (other_ref, other_hot_ref))
    block = min(PATH_BLOCK, paths_ref.shape[0])
    for b in range(paths_ref.shape[0] // block):
        net = net_block(paths_ref[b * block : (b + 1) * block, :], split_ref, trades)
        net_ref[:, b * DATES * block : (b + 1) * DATES * block] = net


def far_kernel(
    paths_ref, split_ref, used_ref, other_ref, onehot_ref, other_hot_ref, near_ref, kept_ref, sent_ref
):
    half = kept_ref.shape[0]
    width = near_ref.shape[1]
    kept_ref[:, :width] = near_ref[:half, :]
    sent_ref[:, :width] = near_ref[half:, :]
    trades = ((used_ref, onehot_ref), (other_ref, other_hot_ref))
    block = min(PATH_BLOCK, paths_ref.shape[0])
    for b in range(paths_ref.shape[0] // block):
        net = net_block(paths_ref[b * block : (b + 1) * block, :], split_ref, trades)
        at = width + b * DATES * block
        kept_ref[:, at : at + DATES * block] = net[:half, :]
        sent_ref[:, at : at + DATES * block] = net[half:, :]


def body(
    factors,
    loadings,
    trade_coef,
    basis_size,
    set_ids,
    live_count,
    netting_row,
    threshold,
    margin_start,
    *,
    count,
):
    me = lax.axis_index("trade")
    own_rows = threshold.shape[0]
    set_total = netting_row.shape[0]
    slot_total, width = trade_coef.shape
    shape = jax.ShapeDtypeStruct
    f32, bf16 = jnp.float32, jnp.bfloat16

    sizes = basis_size.reshape(-1, LANES)
    ids = set_ids.reshape(-1, LANES)
    owner = netting_row.reshape(1, -1)
    turned = loadings.T
    own, used, ids, owner, margin, turned, limits = call(
        fetch_kernel,
        [
            shape(factors.shape, bf16),
            shape(trade_coef.shape, bf16),
            shape(ids.shape, jnp.int32),
            shape(owner.shape, jnp.int32),
            shape(margin_start.shape, f32),
            shape(turned.shape, f32),
            shape((own_rows, LANES), f32),
        ],
        [HBM] * 8,
        10**8,
        tuple(map(in_hbm, (factors, trade_coef, sizes, ids, owner, margin_start, threshold, turned))),
        [
            pltpu.VMEM(trade_coef.shape, bf16),
            pltpu.VMEM(sizes.shape, jnp.int32),
            pltpu.SMEM(threshold.shape, f32),
            pltpu.SemaphoreType.DMA((PARTS + 7,)),
        ],
    )
    near = join(own, swap(factors, 2, count), 2)
    used, ids, live_count, near = lax.optimization_barrier((used, ids, live_count, near))
    other = swap(used, 1, count)
    set_at, onehot, code, held, split = call(
        lambda *refs: rows_kernel(count, own_rows, *refs),
        [
            shape((set_total, LANES), jnp.int32),
            shape((set_total, slot_total), bf16),
            shape(ids.shape, jnp.int32),
            shape((own_rows, DATES * margin_start.shape[1]), f32),
            shape((3, DATES * F, DATES * K), bf16),
        ],
        [SMEM] * 2 + [VMEM] * 4,
        0,
        (me.astype(jnp.int32).reshape(1), live_count, ids, owner, margin, turned),
    )
    (other_hot,) = call(
        other_rows_kernel,
        [shape((set_total, slot_total), bf16)],
        [VMEM] * 2,
        10**8,
        (set_at, swap(code, 1, count)),
    )
    bit = 4
    while bit < count // 2:
        near = join(near, swap(near, bit, count), bit)
        bit *= 2
    far = swap(near, bit, count)
    side_total = near.shape[0]
    columns = DATES * side_total
    work = 4 * columns * slot_total * (width + set_total)
    (near_net,) = call(
        near_kernel,
        [shape((set_total, columns), f32)],
        [VMEM] * 6,
        work,
        (near, split, used, other, onehot, other_hot),
    )
    kept, sent = call(
        far_kernel,
        [shape((set_total // 2, 2 * columns), f32)] * 2,
        [VMEM] * 7,
        work,
        (far, split, used, other, onehot, other_hot, near_net),
    )
    own_net, other_net = scatter_sums(kept, sent, count)
    (own_total,) = call(
        own_kernel,
        [shape((own_rows, DATES * min(PATH_BLOCK, side_total)), f32)],
        [VMEM] * 3,
        10**6,
        (own_net, held, limits),
    )
    (expected,) = call(
        final_kernel,
        [shape((own_rows, DATES), f32)],
        [VMEM] * 4,
        10**6,
        (other_net, held, limits, own_total),
    )
    return expected


def solution(mesh):
    count = mesh.shape["trade"]

    def local(*args):
        return body(*args, count=count)

    return jax.shard_map(
        local,
        mesh=mesh,
        in_specs=(
            P(("group", "trade"), None),
            P(),
            P(("group", "trade"), None),
            P(("group", "trade")),
            P(("group", "trade")),
            P(("group", "trade")),
            P("group"),
            P(("group", "trade")),
            P(("group", "trade"), None),
        ),
        out_specs=P(("group", "trade"), None),
        check_vma=False,
    )
```

```python
import jax
import jax.numpy as jnp
from jax import lax
from jax.experimental import pallas as pl
from jax.experimental.pallas import tpu as pltpu
from jax.sharding import PartitionSpec as P

F = 16
K = 32
DATES = 8
LAG = 2
LANES = 128
PATH_BLOCK = 32
VMEM = pl.BlockSpec(memory_space=pltpu.VMEM)
SMEM = pl.BlockSpec(memory_space=pltpu.SMEM)
HBM = pl.BlockSpec(memory_space=pltpu.HBM)
PARTS = 2


def call(kernel, outs, specs, flops, args, scratch=()):
    sizes = [a.size * a.dtype.itemsize for a in (*args, *outs)]
    return pl.pallas_call(
        kernel,
        out_shape=outs,
        in_specs=specs,
        out_specs=[VMEM] * len(outs),
        scratch_shapes=scratch,
        compiler_params=pltpu.CompilerParams(vmem_limit_bytes=24 * 2**20),
        cost_estimate=pl.CostEstimate(flops=flops, bytes_accessed=sum(sizes) if flops else 0, transcendentals=0),
    )(*args)


def in_hbm(x):
    return pltpu.with_memory_space_constraint(x, pltpu.HBM)


def swap(x, bit, count):
    return lax.ppermute(x, "trade", [(i, i ^ (bit | 1)) for i in range(count)])


def join(own, other, bit):
    upper = (lax.axis_index("trade") & bit) != 0
    return jnp.concatenate([jnp.where(upper, other, own), jnp.where(upper, own, other)], axis=0)


def rounds(count):
    bits = []
    bit = 2
    while bit < count:
        bits.append(bit)
        bit *= 2
    return bits + [1]


def offsets(index, count):
    result = jnp.zeros_like(index)
    top = count // 2
    for bit in rounds(count):
        result = result ^ jnp.where((index & top) != 0, bit | 1, 0)
        top //= 2
    return result


def parity(index, count):
    result = index & 1
    bit = 2
    while bit < count:
        result = result ^ jnp.where((index & bit) != 0, 1, 0)
        bit *= 2
    return result


def scatter_sums(kept, sent, count):
    near = kept.shape[1] // 2
    for bit in rounds(count)[:-1]:
        if bit == count // 2:
            sent = jnp.concatenate([sent[:, near:], sent[:, :near]], axis=1)
        x = kept + swap(sent, bit, count)
        half = x.shape[0] // 2
        kept, sent = x[:half], x[half:]
    return kept, swap(sent, 1, count)


def fetch_kernel(
    factors_hbm,
    coef_hbm,
    size_hbm,
    ids_hbm,
    owner_hbm,
    margin_hbm,
    limit_hbm,
    loadings_hbm,
    own_ref,
    used_ref,
    ids_ref,
    owner_ref,
    margin_ref,
    loadings_ref,
    limits_ref,
    coef_ref,
    size_ref,
    limit_ref,
    sems,
):
    slots, width = coef_ref.shape
    step = slots // PARTS
    pairs = (
        (size_hbm, size_ref),
        (limit_hbm, limit_ref),
        (loadings_hbm, loadings_ref),
        (factors_hbm, own_ref),
        (ids_hbm, ids_ref),
        (owner_hbm, owner_ref),
        (margin_hbm, margin_ref),
    )
    small = [pltpu.make_async_copy(source, target, sems.at[PARTS + i]) for i, (source, target) in enumerate(pairs)]
    large = [
        pltpu.make_async_copy(
            coef_hbm.at[pl.ds(i * step, step), :], coef_ref.at[pl.ds(i * step, step), :], sems.at[i]
        )
        for i in range(PARTS)
    ]
    for copy in small[:3] + large + small[3:]:
        copy.start()
    small[0].wait()
    sizes = size_ref[...].astype(jnp.float32).T
    basis = (lax.broadcasted_iota(jnp.int32, (1, width), 1) & (K - 1)).astype(jnp.float32).astype(jnp.bfloat16)
    for i in range(PARTS):
        large[i].wait()
        for c in range(i * step // LANES, (i + 1) * step // LANES):
            rows = slice(c * LANES, (c + 1) * LANES)
            coef = coef_ref[rows, :]
            used_ref[rows, :] = jnp.where(basis < sizes[:, c : c + 1], coef, jnp.zeros_like(coef))
    for copy in small[1:]:
        copy.wait()
    for r in range(limits_ref.shape[0]):
        limits_ref[r : r + 1, :] = jnp.full((1, LANES), limit_ref[r])


def write_onehot(code, set_at, hot_ref):
    for c in range(code.shape[0]):
        hit = jnp.where(code[c : c + 1, :] == set_at, 1.0, 0.0)
        hot_ref[:, c * LANES : (c + 1) * LANES] = hit.astype(jnp.bfloat16)


def held_margin(count, me, margin, held_ref):
    path_total = margin.shape[1]
    own = path_total // count
    side = path_total // 4
    block = min(PATH_BLOCK, side)
    columns = DATES * block
    lane = lax.broadcasted_iota(jnp.int32, (1, columns), 1)
    source = lax.broadcasted_iota(jnp.int32, (path_total, 1), 0)
    mine = parity(me, count)
    far_bit = jnp.where((me & (count // 2)) != 0, 1, 0)
    inner = lane - (lane // block) * block
    at = 0
    for other in range(2):
        for half in range(2):
            for b in range(side // block):
                place = b * block + inner
                device = place // own
                chip = (far_bit ^ half) * (count // 4) + device
                core = parity(chip, count) ^ mine ^ other
                wanted = (2 * chip + core) * own + (place - device * own)
                pick = jnp.where(source == wanted, 1.0, 0.0)
                held_ref[:, at : at + columns] = jnp.dot(
                    margin, pick, precision=lax.Precision.HIGHEST, preferred_element_type=jnp.float32
                )
                at += columns


def shortfall(net_ref, held_ref, limits_ref, at):
    rows, width = net_ref.shape
    block = min(PATH_BLOCK, width // (2 * DATES))
    columns = DATES * block
    limit = jnp.broadcast_to(limits_ref[:, :1], (rows, columns))
    lane = lax.broadcasted_iota(jnp.int32, (rows, columns), 1)
    total = jnp.zeros((rows, columns), jnp.float32)
    for b in range(width // columns):
        netted = net_ref[:, b * columns : (b + 1) * columns]
        margin = jnp.maximum(pltpu.roll(netted, LAG * block, 1) - limit, 0.0)
        held = held_ref[:, at + b * columns : at + (b + 1) * columns]
        collateral = jnp.where(lane < LAG * block, held, margin)
        total = total + jnp.maximum(netted - collateral, 0.0)
    return total


def own_kernel(own_ref, held_ref, limits_ref, total_ref):
    total_ref[...] = shortfall(own_ref, held_ref, limits_ref, 0)


def final_kernel(other_ref, held_ref, limits_ref, own_ref, out_ref):
    rows, width = other_ref.shape
    columns = own_ref.shape[1]
    rest = own_ref[...] + shortfall(other_ref, held_ref, limits_ref, width)
    date = lax.broadcasted_iota(jnp.int32, (columns, DATES), 0) // (columns // DATES)
    pick = jnp.where(date == lax.broadcasted_iota(jnp.int32, (columns, DATES), 1), 1.0, 0.0).astype(jnp.bfloat16)
    out = jnp.zeros((rows, DATES), jnp.float32)
    for _ in range(3):
        part = rest.astype(jnp.bfloat16)
        out = out + jnp.dot(part, pick, preferred_element_type=jnp.float32)
        rest = rest - part.astype(jnp.float32)
    out_ref[...] = out / (2 * width // DATES)


def rows_kernel(
    count,
    own_rows,
    me_ref,
    live_ref,
    ids_ref,
    owner_ref,
    margin_ref,
    loadings_ref,
    set_ref,
    hot_ref,
    code_ref,
    held_ref,
    split_ref,
):
    held_margin(count, me_ref[0], margin_ref[...], held_ref)
    tall = jnp.concatenate([loadings_ref[...]] * DATES, axis=0)
    wide = jnp.concatenate([tall] * DATES, axis=1)
    row = lax.broadcasted_iota(jnp.int32, wide.shape, 0) // F
    column = lax.broadcasted_iota(jnp.int32, wide.shape, 1) // K
    rest = jnp.where(row == column, wide, 0.0)
    for i in range(3):
        part = rest.astype(jnp.bfloat16)
        split_ref[i] = part
        rest = rest - part.astype(jnp.float32)
    set_total = owner_ref.shape[1]
    place = lax.broadcasted_iota(jnp.int32, (set_total, 1), 0)
    block = lax.shift_right_logical(place, own_rows.bit_length() - 1)
    row_at = (offsets(block, count) ^ me_ref[0]) * own_rows + (place & (own_rows - 1))
    sets = lax.broadcasted_iota(jnp.int32, (set_total, set_total), 1)
    set_at = jnp.sum(jnp.where(row_at == owner_ref[...], sets, 0), axis=1, keepdims=True)
    set_ref[...] = jnp.broadcast_to(set_at, set_ref.shape)
    shape = ids_ref.shape
    slot = lax.broadcasted_iota(jnp.int32, shape, 0) * LANES + lax.broadcasted_iota(jnp.int32, shape, 1)
    code = jnp.where(slot < live_ref[0], ids_ref[...], -1)
    code_ref[...] = code
    write_onehot(code, set_at, hot_ref)


def net_block(paths, split_ref, trades):
    total = paths.shape[0]
    loaded = sum(jnp.dot(paths, split_ref[i], preferred_element_type=jnp.float32) for i in (2, 1, 0))
    tiled = jnp.concatenate([jnp.tanh(loaded)] * DATES, axis=0)
    row = lax.broadcasted_iota(jnp.int32, tiled.shape, 0) // total
    column = lax.broadcasted_iota(jnp.int32, tiled.shape, 1) // K
    table = jnp.where(row == column, tiled, 0.0).astype(jnp.bfloat16)
    result = 0.0
    for used_ref, onehot_ref in trades:
        values = lax.dot_general(
            used_ref[...],
            table,
            (((1,), (1,)), ((), ())),
            preferred_element_type=jnp.float32,
        )
        values = values.astype(jnp.bfloat16)
        result = result + jnp.dot(onehot_ref[...], values, preferred_element_type=jnp.float32)
    return result


def near_kernel(paths_ref, split_ref, used_ref, other_ref, onehot_ref, set_ref, code_ref, net_ref, other_hot_ref):
    write_onehot(code_ref[...], set_ref[:, :1], other_hot_ref)
    trades = ((used_ref, onehot_ref), (other_ref, other_hot_ref))
    block = min(PATH_BLOCK, paths_ref.shape[0])
    for b in range(paths_ref.shape[0] // block):
        net = net_block(paths_ref[b * block : (b + 1) * block, :], split_ref, trades)
        net_ref[:, b * DATES * block : (b + 1) * DATES * block] = net


def far_kernel(
    paths_ref, split_ref, used_ref, other_ref, onehot_ref, other_hot_ref, near_ref, kept_ref, sent_ref
):
    half = kept_ref.shape[0]
    width = near_ref.shape[1]
    kept_ref[:, :width] = near_ref[:half, :]
    sent_ref[:, :width] = near_ref[half:, :]
    trades = ((used_ref, onehot_ref), (other_ref, other_hot_ref))
    block = min(PATH_BLOCK, paths_ref.shape[0])
    for b in range(paths_ref.shape[0] // block):
        net = net_block(paths_ref[b * block : (b + 1) * block, :], split_ref, trades)
        at = width + b * DATES * block
        kept_ref[:, at : at + DATES * block] = net[:half, :]
        sent_ref[:, at : at + DATES * block] = net[half:, :]


def body(
    factors,
    loadings,
    trade_coef,
    basis_size,
    set_ids,
    live_count,
    netting_row,
    threshold,
    margin_start,
    *,
    count,
):
    me = lax.axis_index("trade")
    own_rows = threshold.shape[0]
    set_total = netting_row.shape[0]
    slot_total, width = trade_coef.shape
    shape = jax.ShapeDtypeStruct
    f32, bf16 = jnp.float32, jnp.bfloat16

    sizes = basis_size.reshape(-1, LANES)
    ids = set_ids.reshape(-1, LANES)
    owner = netting_row.reshape(1, -1)
    turned = loadings.T
    own, used, ids, owner, margin, turned, limits = call(
        fetch_kernel,
        [
            shape(factors.shape, bf16),
            shape(trade_coef.shape, bf16),
            shape(ids.shape, jnp.int32),
            shape(owner.shape, jnp.int32),
            shape(margin_start.shape, f32),
            shape(turned.shape, f32),
            shape((own_rows, LANES), f32),
        ],
        [HBM] * 8,
        10**8,
        tuple(map(in_hbm, (factors, trade_coef, sizes, ids, owner, margin_start, threshold, turned))),
        [
            pltpu.VMEM(trade_coef.shape, bf16),
            pltpu.VMEM(sizes.shape, jnp.int32),
            pltpu.SMEM(threshold.shape, f32),
            pltpu.SemaphoreType.DMA((PARTS + 7,)),
        ],
    )
    near = join(own, swap(factors, 2, count), 2)
    used, ids, live_count, near = lax.optimization_barrier((used, ids, live_count, near))
    other = swap(used, 1, count)
    set_at, onehot, code, held, split = call(
        lambda *refs: rows_kernel(count, own_rows, *refs),
        [
            shape((set_total, LANES), jnp.int32),
            shape((set_total, slot_total), bf16),
            shape(ids.shape, jnp.int32),
            shape((own_rows, DATES * margin_start.shape[1]), f32),
            shape((3, DATES * F, DATES * K), bf16),
        ],
        [SMEM] * 2 + [VMEM] * 4,
        0,
        (me.astype(jnp.int32).reshape(1), live_count, ids, owner, margin, turned),
    )
    other_code = swap(code, 1, count)
    bit = 4
    while bit < count // 2:
        near = join(near, swap(near, bit, count), bit)
        bit *= 2
    far = swap(near, bit, count)
    side_total = near.shape[0]
    columns = DATES * side_total
    work = 4 * columns * slot_total * (width + set_total)
    near_net, other_hot = call(
        near_kernel,
        [shape((set_total, columns), f32), shape((set_total, slot_total), bf16)],
        [VMEM] * 7,
        work,
        (near, split, used, other, onehot, set_at, other_code),
    )
    kept, sent = call(
        far_kernel,
        [shape((set_total // 2, 2 * columns), f32)] * 2,
        [VMEM] * 7,
        work,
        (far, split, used, other, onehot, other_hot, near_net),
    )
    own_net, other_net = scatter_sums(kept, sent, count)
    (own_total,) = call(
        own_kernel,
        [shape((own_rows, DATES * min(PATH_BLOCK, side_total)), f32)],
        [VMEM] * 3,
        10**6,
        (own_net, held, limits),
    )
    (expected,) = call(
        final_kernel,
        [shape((own_rows, DATES), f32)],
        [VMEM] * 4,
        10**6,
        (other_net, held, limits, own_total),
    )
    return expected


def solution(mesh):
    count = mesh.shape["trade"]

    def local(*args):
        return body(*args, count=count)

    return jax.shard_map(
        local,
        mesh=mesh,
        in_specs=(
            P(("group", "trade"), None),
            P(),
            P(("group", "trade"), None),
            P(("group", "trade")),
            P(("group", "trade")),
            P(("group", "trade")),
            P("group"),
            P(("group", "trade")),
            P(("group", "trade"), None),
        ),
        out_specs=P(("group", "trade"), None),
        check_vma=False,
    )
```
